256 devices in a mesh: wa: 32 (over x, y, core), an: 8 (over z).
Axes of the slice: x: 4, y: 4, z: 8, core: 2. Of those that a mesh axis runs over, the one named last changes fastest.
Arguments:
- tensor: float32 [256, 1024, 128, 4], P('wa', None, 'an'), may hold values from -6 to 6
- factor_two: float32 [1024, 64], P('wa'), may hold values from -0.1875 to 0.1875
- factor_three: float32 [128, 64], P('an'), may hold values from -0.5 to 0.5
- factor_four: float32 [4, 2], replicated, may hold values from -3 to 3
- start_basis: float32 [256, 64], P('wa'), may hold values from -0.375 to 0.375
Outputs:
- scaled_factor: float32 [256, 64], P('wa')
The draws below stay inside these ranges and needn't reach their ends.
All inputs are finite; a program needn't handle non-finite values.
Results may differ from the reference program's by a relative error of at most 0.00024.
Values sent between devices are 32-bit elements; how exact they have to be, the bound alone decides.
A program may use at most 64 MiB of HBM per device.

```python
import math
import jax
import jax.numpy as jnp
from jax import lax

MODE_TWO = 1024
MODE_FOUR = 4
RANK = 64
RANK_FOUR = 2
ITERS = 4
MODE_ONE = 256
MODE_THREE = 128


def block_levels(stream_key, extent, shards, least, top_value):
    def one(axis_at, shards_of):
        heights = jax.random.uniform(jax.random.fold_in(jax.random.fold_in(stream_key, 6), axis_at), (shards_of,), jnp.float32, least / len(shards), top_value / len(shards))
        return jnp.repeat(jnp.exp(heights), extent[axis_at] // shards_of).reshape((-1,) + (1,) * (len(extent) - axis_at - 1))

    level = one(*shards[0])
    for cut in shards[1:]:
        level = level * one(*cut)
    return level


def normal_values(stream_key, shape, deviation, most, shards=(), held_as=jnp.bfloat16):
    drawn = jax.random.normal(stream_key, shape, jnp.float32) * deviation
    if len(shards) > 0:
        drawn = block_levels(stream_key, shape, shards, -0.22, 0.18) * drawn
    return jnp.clip(drawn, min=-most, max=most).astype(held_as)


def setup_inputs(seed: int = 0) -> dict:
    keys = jax.random.split(jax.random.key(seed), 6)
    return {
        "tensor": normal_values(keys[0], (MODE_ONE, MODE_TWO, MODE_THREE, MODE_FOUR), 1.0, 6.0, ((0, 32), (2, 8)), jnp.float32),
        "factor_two": normal_values(keys[1], (MODE_TWO, RANK), MODE_TWO ** -0.5, 0.1875, ((0, 32),), jnp.float32),
        "factor_three": normal_values(keys[2], (MODE_THREE, RANK), MODE_THREE ** -0.5, 0.5, ((0, 8),), jnp.float32),
        "factor_four": normal_values(keys[3], (MODE_FOUR, RANK_FOUR), MODE_FOUR ** -0.5, 3.0, (), jnp.float32),
        "start_basis": normal_values(keys[4], (MODE_ONE, RANK), MODE_ONE ** -0.5, 0.375, ((0, 32),), jnp.float32),
    }


def reference(tensor, factor_two, factor_three, factor_four, start_basis):
    highest = lax.Precision.HIGHEST
    first = jnp.einsum('abcd,be->aecd', tensor, factor_two, precision=highest)
    second = jnp.einsum('aecd,cf->aefd', first, factor_three, precision=highest)
    core = jnp.einsum('aefd,dg->aefg', second, factor_four, precision=highest)
    unfold = core.reshape(core.shape[0], -1)
    gram = jnp.dot(unfold.astype(jnp.float32), unfold.T.astype(jnp.float32), precision=highest, preferred_element_type=jnp.float32)
    gram = gram / float(RANK * RANK * RANK_FOUR)
    basis = start_basis
    for step in range(ITERS):
        image = jnp.dot(gram.astype(jnp.float32), basis.astype(jnp.float32), precision=highest, preferred_element_type=jnp.float32)
        small = jnp.dot(image.T.astype(jnp.float32), image.astype(jnp.float32), precision=highest, preferred_element_type=jnp.float32)
        lower = jnp.linalg.cholesky(small)
        basis = lax.linalg.triangular_solve(lower, image, left_side=False, lower=True, transpose_a=True)
    return basis * math.sqrt(MODE_ONE)
```

```python
import functools
import math

import jax
import jax.numpy as jnp
from jax import lax
from jax.experimental import pallas as pl
from jax.experimental.pallas import tpu as pltpu
from jax.sharding import PartitionSpec as P

RANK = 64
RANK_FOUR = 2
ITERS = 4
NW, NZ = 32, 8
CHIPS = NW // 2
BLOCK = 8
MESH = pl.DeviceIdType.MESH
HIGHEST = lax.Precision.HIGHEST


def split3(x):
    h = x.astype(jnp.bfloat16)
    rest = x - h.astype(jnp.float32)
    m = rest.astype(jnp.bfloat16)
    l = (rest - m.astype(jnp.float32)).astype(jnp.bfloat16)
    return h, m, l


def mm(a, b, dims=((1,), (0,))):
    return lax.dot_general(
        a, b, (dims, ((), ())), precision=HIGHEST, preferred_element_type=jnp.float32
    )


def mm16(a, b):
    return jnp.dot(a, b, preferred_element_type=jnp.float32)


def lanes_of(tile, column):
    return jnp.broadcast_to(tile[:, column : column + 1], (8, 128))


def rows_of(tile, row):
    return jnp.broadcast_to(tile[row : row + 1, :], (8, 128))


def inverse_cholesky(w):
    row = lax.broadcasted_iota(jnp.int32, (8, 128), 0)
    lane = lax.broadcasted_iota(jnp.int32, (8, 128), 1)
    wide = jnp.concatenate([w, jnp.zeros((64, 64), jnp.float32)], axis=1)
    s = []
    for i in range(8):
        unit = jnp.where(lane == row + (64 + 8 * i), 1.0, 0.0)
        s.append(jnp.where(lane < 64, wide[8 * i : 8 * i + 8], unit))
    out = []
    for t in range(8):
        pivots = jnp.ones((8, 128), jnp.float32)
        for start in range(0, 8, BLOCK):
            cols = {
                i: [lanes_of(s[i], 8 * t + start + q) for q in range(BLOCK)]
                for i in range(t, 8)
            }
            for p in range(BLOCK):
                r = start + p
                pivot_row = rows_of(s[t], r)
                pivot = rows_of(cols[t][p], r)
                inverse = 1.0 / pivot
                heads = [rows_of(cols[t][q], r) for q in range(BLOCK)]
                for i in range(t, 8):
                    factor = cols[i][p] * inverse
                    if i == t:
                        factor = jnp.where(row > r, factor, 0.0)
                    s[i] = s[i] - factor * pivot_row
                    for q in range(p + 1, BLOCK):
                        cols[i][q] = cols[i][q] - factor * heads[q]
                pivots = jnp.where(row == r, pivot, pivots)
        out.append(s[t] * lax.rsqrt(pivots))
    return jnp.concatenate(out, axis=0)[:, 64:128]


def kernel(
    x_hbm, f2_hbm, f3_hbm, f4_hbm, b0_hbm, out_ref,
    xv, f2v, f3v, f4s, b0v, f2p, f2g, f3g, b0g, yh, ym, yl,
    s1, r1, vt, v_ref, a_ref, gp, g3, gsum, gfull, z_ref, linv_ref,
    loc, snd, rcv,
):
    w = lax.axis_index("wa")
    n = lax.axis_index("an")
    core = lax.rem(w, 2)
    chip = w // 2

    local = [
        pltpu.make_async_copy(f2_hbm, f2v, loc.at[0]),
        pltpu.make_async_copy(f3_hbm, f3v, loc.at[1]),
        pltpu.make_async_copy(b0_hbm, b0v, loc.at[2]),
        pltpu.make_async_copy(f4_hbm, f4s, loc.at[3]),
        pltpu.make_async_copy(x_hbm, xv, loc.at[4]),
    ]
    for copy in local:
        copy.start()

    barrier = pltpu.get_barrier_semaphore()

    def plane_peer(k):
        return lax.rem(w + k, NW), n

    def column_peer(k):
        return chip * 2 + lax.rem(core + k, 2), lax.rem(n + k // 2, NZ)

    @pl.loop(1, NW)
    def _(k):
        pl.semaphore_signal(barrier, inc=1, device_id=plane_peer(k), device_id_type=MESH)

    @pl.loop(2, 2 * NZ)
    def _(k):
        pl.semaphore_signal(barrier, inc=1, device_id=column_peer(k), device_id_type=MESH)

    local[0].wait()
    local[1].wait()
    local[2].wait()
    f2p[:, 0:64] = f2v[0:16, :]
    f2p[:, 64:128] = f2v[16:32, :]
    f2g[w] = f2p[...]
    f3g[n] = f3v[...]
    b0g[w] = b0v[...]

    pl.semaphore_wait(barrier, NW - 1 + 2 * NZ - 2)

    def send(stage, src, dst, peer):
        pltpu.make_async_remote_copy(
            src_ref=src, dst_ref=dst, send_sem=snd.at[stage], recv_sem=rcv.at[stage],
            device_id=peer, device_id_type=MESH,
        ).start()

    def await_all(sem, blocks):
        pltpu.make_async_copy(blocks, blocks, sem).wait()

    @pl.loop(1, NW)
    def _(k):
        send(0, f2p, f2g.at[w], plane_peer(k))

    @pl.loop(1, NZ)
    def _(k):
        send(1, f3v, f3g.at[n], (w, lax.rem(n + k, NZ)))

    @pl.loop(1, NW)
    def _(k):
        send(2, b0v, b0g.at[w], plane_peer(k))

    local[3].wait()
    local[4].wait()
    for bt in range(8):
        parts = [xv[pl.ds(bt * 4 + d, 128, stride=32), :] for d in range(4)]
        for g in range(2):
            total = parts[0] * f4s[g, 0]
            for d in range(1, 4):
                total = total + parts[d] * f4s[g, d]
            h, m, l = split3(total)
            here = (slice(128 * g, 128 * g + 128), slice(128 * bt, 128 * bt + 128))
            yh[here] = h
            ym[here] = m
            yl[here] = l

    await_all(rcv.at[0], f2g.at[pl.ds(0, NW - 1)])
    packed = f2g[...]
    full_two = jnp.concatenate([packed[:, :, 0:64], packed[:, :, 64:128]], axis=1)
    wh, wm, wl = split3(full_two.reshape(1024, 64))
    p0 = mm16(yh[...], jnp.concatenate([wh, wm, wl], axis=1))
    p1 = mm16(ym[...], jnp.concatenate([wh, wm], axis=1))
    p2 = mm16(yl[...], wh)
    first = (p0[:, 128:192] + p1[:, 64:128] + p2) + (p0[:, 64:128] + p1[:, 0:64]) + p0[:, 0:64]
    for g in range(2):
        s1[g] = first[128 * g : 128 * g + 128].T.reshape(8, 8, 128)

    @pl.loop(1, 2 * NZ)
    def _(k):
        to_w, to_n = column_peer(k)
        send(3, s1.at[lax.rem(to_w, 2), to_n], r1.at[core * NZ + n], (to_w, to_n))

    r1[core * NZ + n] = s1[core, n]
    await_all(rcv.at[1], f3g.at[pl.ds(0, NZ - 1)])
    full_three = f3g[...].reshape(128, 64)
    await_all(rcv.at[3], r1.at[pl.ds(0, 2 * NZ - 1)])

    lane = lax.broadcasted_iota(jnp.int32, (8, 128), 1)
    rows = []
    for s in range(2):
        v = [r1[s * NZ + m] for m in range(NZ)]
        for d in (4, 2, 1):
            upper = lax.rem(lane // (16 * d), 2) == 1
            nxt = list(v)
            for i in range(8):
                if i & d == 0:
                    j = i + d
                    nxt[i] = jnp.where(upper, pltpu.roll(v[j], 16 * d, 1), v[i])
                    nxt[j] = jnp.where(upper, v[j], pltpu.roll(v[i], 128 - 16 * d, 1))
            v = nxt
        rows += v
    vt[...] = mm(jnp.concatenate(rows, axis=0), full_three)
    for e in range(8):
        v_ref[:, 64 * e : 64 * e + 64] = vt[pl.ds(e, 16, stride=8), :]

    @pl.loop(1, CHIPS)
    def _(k):
        send(4, v_ref, a_ref.at[chip], (lax.rem(chip + k, CHIPS) * 2 + core, n))

    a_ref[chip] = v_ref[...]
    await_all(rcv.at[4], a_ref.at[pl.ds(0, CHIPS - 1)])
    partial = mm(v_ref[...], a_ref[...].reshape(256, 512), ((1,), (1,)))
    gp[...] = partial.reshape(2, 8, 256)

    @pl.loop(1, 2 * NZ)
    def _(k):
        to_w, to_n = column_peer(k)
        send(5, gp.at[lax.rem(to_w, 2)], g3.at[core * NZ + n], (to_w, to_n))

    g3[core * NZ + n] = gp[core]
    await_all(rcv.at[5], g3.at[pl.ds(0, 2 * NZ - 1)])
    total = g3[0]
    for i in range(1, 2 * NZ):
        total = total + g3[i]
    gsum[...] = total * (1.0 / float(RANK * RANK * RANK_FOUR))

    @pl.loop(1, NW)
    def _(k):
        send(6, gsum, gfull.at[w], plane_peer(k))

    gfull[w] = gsum[...]
    await_all(rcv.at[2], b0g.at[pl.ds(0, NW - 1)])
    basis = b0g[...].reshape(256, 64)
    await_all(rcv.at[6], gfull.at[pl.ds(0, NW - 1)])

    z_ref[...] = mm(gfull[...].reshape(256, 256), basis)

    @pl.loop(0, ITERS)
    def _(step):
        z = z_ref[...]
        linv_ref[...] = inverse_cholesky(mm(z, z, ((0,), (0,))))

        @pl.when(step < ITERS - 1)
        def _():
            image = mm(gfull[...].reshape(256, 256), z)
            z_ref[...] = mm(image, linv_ref[...], ((1,), (1,)))

    mine = z_ref[pl.ds(pl.multiple_of(w * 8, 8), 8), :]
    out_ref[...] = mm(mine, linv_ref[...], ((1,), (1,))) * math.sqrt(256.0)

    await_all(snd.at[0], f2g.at[pl.ds(0, NW - 1)])
    await_all(snd.at[1], f3g.at[pl.ds(0, NZ - 1)])
    await_all(snd.at[2], b0g.at[pl.ds(0, NW - 1)])
    await_all(snd.at[3], r1.at[pl.ds(0, 2 * NZ - 1)])
    await_all(snd.at[4], a_ref.at[pl.ds(0, CHIPS - 1)])
    await_all(snd.at[5], g3.at[pl.ds(0, 2 * NZ - 1)])
    await_all(snd.at[6], gfull.at[pl.ds(0, NW - 1)])


def per_device(tensor, factor_two, factor_three, factor_four, start_basis):
    f32, bf16 = jnp.float32, jnp.bfloat16
    x = tensor.reshape(8, 8, 128, 16, 4).transpose(0, 3, 1, 4, 2).reshape(4096, 128)
    hbm = pl.BlockSpec(memory_space=pltpu.HBM)
    return pl.pallas_call(
        kernel,
        out_shape=jax.ShapeDtypeStruct((8, 64), f32),
        in_specs=[hbm] * 5,
        out_specs=pl.BlockSpec(memory_space=pltpu.VMEM),
        scratch_shapes=[
            pltpu.VMEM((4096, 128), f32),
            pltpu.VMEM((32, 64), f32),
            pltpu.VMEM((16, 64), f32),
            pltpu.SMEM((2, 4), f32),
            pltpu.VMEM((8, 64), f32),
            pltpu.VMEM((16, 128), f32),
            pltpu.VMEM((NW, 16, 128), f32),
            pltpu.VMEM((NZ, 16, 64), f32),
            pltpu.VMEM((NW, 8, 64), f32),
            pltpu.VMEM((256, 1024), bf16),
            pltpu.VMEM((256, 1024), bf16),
            pltpu.VMEM((256, 1024), bf16),
            pltpu.VMEM((2, 8, 8, 128), f32),
            pltpu.VMEM((16, 8, 128), f32),
            pltpu.VMEM((128, 64), f32),
            pltpu.VMEM((16, 512), f32),
            pltpu.VMEM((CHIPS, 16, 512), f32),
            pltpu.VMEM((2, 8, 256), f32),
            pltpu.VMEM((16, 8, 256), f32),
            pltpu.VMEM((8, 256), f32),
            pltpu.VMEM((NW, 8, 256), f32),
            pltpu.VMEM((256, 64), f32),
            pltpu.VMEM((64, 64), f32),
            pltpu.SemaphoreType.DMA((5,)),
            pltpu.SemaphoreType.DMA((7,)),
            pltpu.SemaphoreType.DMA((7,)),
        ],
        compiler_params=pltpu.CompilerParams(
            collective_id=0, has_side_effects=True, vmem_limit_bytes=40 * 2**20
        ),
        name="hooi",
    )(x, factor_two, factor_three, factor_four.T, start_basis)


def solution(mesh):
    in_specs = (P("wa", None, "an", None), P("wa", None), P("an", None), P(), P("wa", None))
    return jax.shard_map(
        per_device, mesh=mesh, in_specs=in_specs, out_specs=P("wa", None), check_vma=False
    )
```

```python
import functools
import math

import jax
import jax.numpy as jnp
from jax import lax
from jax.experimental import pallas as pl
from jax.experimental.pallas import tpu as pltpu
from jax.sharding import PartitionSpec as P

RANK = 64
RANK_FOUR = 2
ITERS = 4
NW, NZ = 32, 8
CHIPS = NW // 2
BLOCK = 8
MESH = pl.DeviceIdType.MESH
HIGHEST = lax.Precision.HIGHEST


def split3(x):
    h = x.astype(jnp.bfloat16)
    rest = x - h.astype(jnp.float32)
    m = rest.astype(jnp.bfloat16)
    l = (rest - m.astype(jnp.float32)).astype(jnp.bfloat16)
    return h, m, l


def mm(a, b, dims=((1,), (0,))):
    return lax.dot_general(
        a, b, (dims, ((), ())), precision=HIGHEST, preferred_element_type=jnp.float32
    )


def mm16(a, b):
    return jnp.dot(a, b, preferred_element_type=jnp.float32)


def lanes_of(tile, column):
    return jnp.broadcast_to(tile[:, column : column + 1], (8, 128))


def rows_of(tile, row):
    return jnp.broadcast_to(tile[row : row + 1, :], (8, 128))


def inverse_cholesky(w):
    row = lax.broadcasted_iota(jnp.int32, (8, 128), 0)
    lane = lax.broadcasted_iota(jnp.int32, (8, 128), 1)
    wide = jnp.concatenate([w, jnp.zeros((64, 64), jnp.float32)], axis=1)
    s = []
    for i in range(8):
        unit = jnp.where(lane == row + (64 + 8 * i), 1.0, 0.0)
        s.append(jnp.where(lane < 64, wide[8 * i : 8 * i + 8], unit))
    out = []
    for t in range(8):
        pivots = jnp.ones((8, 128), jnp.float32)
        for start in range(0, 8, BLOCK):
            cols = {
                i: [lanes_of(s[i], 8 * t + start + q) for q in range(BLOCK)]
                for i in range(t, 8)
            }
            for p in range(BLOCK):
                r = start + p
                pivot_row = rows_of(s[t], r)
                pivot = rows_of(cols[t][p], r)
                inverse = 1.0 / pivot
                heads = [rows_of(cols[t][q], r) for q in range(BLOCK)]
                for i in range(t, 8):
                    factor = cols[i][p] * inverse
                    if i == t:
                        factor = jnp.where(row > r, factor, 0.0)
                    s[i] = s[i] - factor * pivot_row
                    for q in range(p + 1, BLOCK):
                        cols[i][q] = cols[i][q] - factor * heads[q]
                pivots = jnp.where(row == r, pivot, pivots)
        out.append(s[t] * lax.rsqrt(pivots))
    return jnp.concatenate(out, axis=0)[:, 64:128]


def kernel(
    x_hbm, f2_hbm, f3_hbm, f4_hbm, b0_hbm, out_ref,
    xv, f2v, f3v, f4s, b0v, f2p, f2g, f3g, b0g, yh, ym, yl,
    s1, r1, vt, v_ref, a_ref, gp, g3, gsum, gfull, z_ref, linv_ref,
    loc, snd, rcv,
):
    w = lax.axis_index("wa")
    n = lax.axis_index("an")
    core = lax.rem(w, 2)
    chip = w // 2

    local = [
        pltpu.make_async_copy(f2_hbm, f2v, loc.at[0]),
        pltpu.make_async_copy(f3_hbm, f3v, loc.at[1]),
        pltpu.make_async_copy(b0_hbm, b0v, loc.at[2]),
        pltpu.make_async_copy(f4_hbm, f4s, loc.at[3]),
        pltpu.make_async_copy(x_hbm, xv, loc.at[4]),
    ]
    for copy in local:
        copy.start()

    barrier = pltpu.get_barrier_semaphore()

    def plane_peer(k):
        return lax.rem(w + k, NW), n

    def column_peer(k):
        return chip * 2 + lax.rem(core + k, 2), lax.rem(n + k // 2, NZ)

    @pl.loop(1, NW)
    def _(k):
        pl.semaphore_signal(barrier, inc=1, device_id=plane_peer(k), device_id_type=MESH)

    @pl.loop(2, 2 * NZ)
    def _(k):
        pl.semaphore_signal(barrier, inc=1, device_id=column_peer(k), device_id_type=MESH)

    local[0].wait()
    local[1].wait()
    local[2].wait()
    f2p[:, 0:64] = f2v[0:16, :]
    f2p[:, 64:128] = f2v[16:32, :]
    f2g[w] = f2p[...]
    f3g[n] = f3v[...]
    b0g[w] = b0v[...]

    local[3].wait()
    local[4].wait()
    for bt in range(8):
        parts = [xv[pl.ds(bt * 4 + d, 128, stride=32), :] for d in range(4)]
        for g in range(2):
            total = parts[0] * f4s[g, 0]
            for d in range(1, 4):
                total = total + parts[d] * f4s[g, d]
            h, m, l = split3(total)
            here = (slice(128 * g, 128 * g + 128), slice(128 * bt, 128 * bt + 128))
            yh[here] = h
            ym[here] = m
            yl[here] = l

    pl.semaphore_wait(barrier, NW - 1 + 2 * NZ - 2)

    def send(stage, src, dst, peer):
        pltpu.make_async_remote_copy(
            src_ref=src, dst_ref=dst, send_sem=snd.at[stage], recv_sem=rcv.at[stage],
            device_id=peer, device_id_type=MESH,
        ).start()

    def await_all(sem, blocks):
        pltpu.make_async_copy(blocks, blocks, sem).wait()

    @pl.loop(1, NW)
    def _(k):
        send(0, f2p, f2g.at[w], plane_peer(k))

    @pl.loop(1, NZ)
    def _(k):
        send(1, f3v, f3g.at[n], (w, lax.rem(n + k, NZ)))

    await_all(rcv.at[0], f2g.at[pl.ds(0, NW - 1)])
    packed = f2g[...]
    full_two = jnp.concatenate([packed[:, :, 0:64], packed[:, :, 64:128]], axis=1)
    wh, wm, wl = split3(full_two.reshape(1024, 64))
    p0 = mm16(yh[...], jnp.concatenate([wh, wm, wl], axis=1))
    p1 = mm16(ym[...], jnp.concatenate([wh, wm], axis=1))
    p2 = mm16(yl[...], wh)
    first = (p0[:, 128:192] + p1[:, 64:128] + p2) + (p0[:, 64:128] + p1[:, 0:64]) + p0[:, 0:64]
    for g in range(2):
        s1[g] = first[128 * g : 128 * g + 128].T.reshape(8, 8, 128)

    @pl.loop(1, 2 * NZ)
    def _(k):
        to_w, to_n = column_peer(k)
        send(3, s1.at[lax.rem(to_w, 2), to_n], r1.at[core * NZ + n], (to_w, to_n))

    @pl.loop(1, NW)
    def _(k):
        send(2, b0v, b0g.at[w], plane_peer(k))

    r1[core * NZ + n] = s1[core, n]
    await_all(rcv.at[1], f3g.at[pl.ds(0, NZ - 1)])
    full_three = f3g[...].reshape(128, 64)
    await_all(rcv.at[3], r1.at[pl.ds(0, 2 * NZ - 1)])

    lane = lax.broadcasted_iota(jnp.int32, (8, 128), 1)
    rows = []
    for s in range(2):
        v = [r1[s * NZ + m] for m in range(NZ)]
        for d in (4, 2, 1):
            upper = lax.rem(lane // (16 * d), 2) == 1
            nxt = list(v)
            for i in range(8):
                if i & d == 0:
                    j = i + d
                    nxt[i] = jnp.where(upper, pltpu.roll(v[j], 16 * d, 1), v[i])
                    nxt[j] = jnp.where(upper, v[j], pltpu.roll(v[i], 128 - 16 * d, 1))
            v = nxt
        rows += v
    vt[...] = mm(jnp.concatenate(rows, axis=0), full_three)
    for e in range(8):
        v_ref[:, 64 * e : 64 * e + 64] = vt[pl.ds(e, 16, stride=8), :]

    @pl.loop(1, CHIPS)
    def _(k):
        send(4, v_ref, a_ref.at[chip], (lax.rem(chip + k, CHIPS) * 2 + core, n))

    a_ref[chip] = v_ref[...]
    await_all(rcv.at[4], a_ref.at[pl.ds(0, CHIPS - 1)])
    partial = mm(v_ref[...], a_ref[...].reshape(256, 512), ((1,), (1,)))
    gp[...] = partial.reshape(2, 8, 256)

    @pl.loop(1, 2 * NZ)
    def _(k):
        to_w, to_n = column_peer(k)
        send(5, gp.at[lax.rem(to_w, 2)], g3.at[core * NZ + n], (to_w, to_n))

    g3[core * NZ + n] = gp[core]
    await_all(rcv.at[5], g3.at[pl.ds(0, 2 * NZ - 1)])
    total = g3[0]
    for i in range(1, 2 * NZ):
        total = total + g3[i]
    gsum[...] = total * (1.0 / float(RANK * RANK * RANK_FOUR))

    @pl.loop(1, NW)
    def _(k):
        send(6, gsum, gfull.at[w], plane_peer(k))

    gfull[w] = gsum[...]
    await_all(rcv.at[2], b0g.at[pl.ds(0, NW - 1)])
    basis = b0g[...].reshape(256, 64)
    await_all(rcv.at[6], gfull.at[pl.ds(0, NW - 1)])

    z_ref[...] = mm(gfull[...].reshape(256, 256), basis)

    @pl.loop(0, ITERS)
    def _(step):
        z = z_ref[...]
        linv_ref[...] = inverse_cholesky(mm(z, z, ((0,), (0,))))

        @pl.when(step < ITERS - 1)
        def _():
            image = mm(gfull[...].reshape(256, 256), z)
            z_ref[...] = mm(image, linv_ref[...], ((1,), (1,)))

    mine = z_ref[pl.ds(pl.multiple_of(w * 8, 8), 8), :]
    out_ref[...] = mm(mine, linv_ref[...], ((1,), (1,))) * math.sqrt(256.0)

    await_all(snd.at[0], f2g.at[pl.ds(0, NW - 1)])
    await_all(snd.at[1], f3g.at[pl.ds(0, NZ - 1)])
    await_all(snd.at[2], b0g.at[pl.ds(0, NW - 1)])
    await_all(snd.at[3], r1.at[pl.ds(0, 2 * NZ - 1)])
    await_all(snd.at[4], a_ref.at[pl.ds(0, CHIPS - 1)])
    await_all(snd.at[5], g3.at[pl.ds(0, 2 * NZ - 1)])
    await_all(snd.at[6], gfull.at[pl.ds(0, NW - 1)])


def per_device(tensor, factor_two, factor_three, factor_four, start_basis):
    f32, bf16 = jnp.float32, jnp.bfloat16
    x = tensor.reshape(8, 8, 128, 16, 4).transpose(0, 3, 1, 4, 2).reshape(4096, 128)
    hbm = pl.BlockSpec(memory_space=pltpu.HBM)
    return pl.pallas_call(
        kernel,
        out_shape=jax.ShapeDtypeStruct((8, 64), f32),
        in_specs=[hbm] * 5,
        out_specs=pl.BlockSpec(memory_space=pltpu.VMEM),
        scratch_shapes=[
            pltpu.VMEM((4096, 128), f32),
            pltpu.VMEM((32, 64), f32),
            pltpu.VMEM((16, 64), f32),
            pltpu.SMEM((2, 4), f32),
            pltpu.VMEM((8, 64), f32),
            pltpu.VMEM((16, 128), f32),
            pltpu.VMEM((NW, 16, 128), f32),
            pltpu.VMEM((NZ, 16, 64), f32),
            pltpu.VMEM((NW, 8, 64), f32),
            pltpu.VMEM((256, 1024), bf16),
            pltpu.VMEM((256, 1024), bf16),
            pltpu.VMEM((256, 1024), bf16),
            pltpu.VMEM((2, 8, 8, 128), f32),
            pltpu.VMEM((16, 8, 128), f32),
            pltpu.VMEM((128, 64), f32),
            pltpu.VMEM((16, 512), f32),
            pltpu.VMEM((CHIPS, 16, 512), f32),
            pltpu.VMEM((2, 8, 256), f32),
            pltpu.VMEM((16, 8, 256), f32),
            pltpu.VMEM((8, 256), f32),
            pltpu.VMEM((NW, 8, 256), f32),
            pltpu.VMEM((256, 64), f32),
            pltpu.VMEM((64, 64), f32),
            pltpu.SemaphoreType.DMA((5,)),
            pltpu.SemaphoreType.DMA((7,)),
            pltpu.SemaphoreType.DMA((7,)),
        ],
        compiler_params=pltpu.CompilerParams(
            collective_id=0, has_side_effects=True, vmem_limit_bytes=60 * 2**20
        ),
        name="hooi",
    )(x, factor_two, factor_three, factor_four.T, start_basis)


def solution(mesh):
    in_specs = (P("wa", None, "an", None), P("wa", None), P("an", None), P(), P("wa", None))
    return jax.shard_map(
        per_device, mesh=mesh, in_specs=in_specs, out_specs=P("wa", None), check_vma=False
    )
```

```python
import functools
import math

import jax
import jax.numpy as jnp
from jax import lax
from jax.experimental import pallas as pl
from jax.experimental.pallas import tpu as pltpu
from jax.sharding import PartitionSpec as P

RANK = 64
RANK_FOUR = 2
ITERS = 4
NW, NZ = 32, 8
CHIPS = NW // 2
HALF = CHIPS // 2
BLOCK = 8
MESH = pl.DeviceIdType.MESH
HIGHEST = lax.Precision.HIGHEST


def split3(x):
    h = x.astype(jnp.bfloat16)
    rest = x - h.astype(jnp.float32)
    m = rest.astype(jnp.bfloat16)
    l = (rest - m.astype(jnp.float32)).astype(jnp.bfloat16)
    return h, m, l


def mm(a, b, dims=((1,), (0,))):
    return lax.dot_general(
        a, b, (dims, ((), ())), precision=HIGHEST, preferred_element_type=jnp.float32
    )


def mm16(a, b):
    return jnp.dot(a, b, preferred_element_type=jnp.float32)


def lanes_of(tile, column):
    return jnp.broadcast_to(tile[:, column : column + 1], (8, 128))


def rows_of(tile, row):
    return jnp.broadcast_to(tile[row : row + 1, :], (8, 128))


def inverse_cholesky(w):
    row = lax.broadcasted_iota(jnp.int32, (8, 128), 0)
    lane = lax.broadcasted_iota(jnp.int32, (8, 128), 1)
    wide = jnp.concatenate([w, jnp.zeros((64, 64), jnp.float32)], axis=1)
    s = []
    for i in range(8):
        unit = jnp.where(lane == row + (64 + 8 * i), 1.0, 0.0)
        s.append(jnp.where(lane < 64, wide[8 * i : 8 * i + 8], unit))
    out = []
    for t in range(8):
        pivots = jnp.ones((8, 128), jnp.float32)
        for start in range(0, 8, BLOCK):
            cols = {
                i: [lanes_of(s[i], 8 * t + start + q) for q in range(BLOCK)]
                for i in range(t, 8)
            }
            for p in range(BLOCK):
                r = start + p
                pivot_row = rows_of(s[t], r)
                pivot = rows_of(cols[t][p], r)
                inverse = 1.0 / pivot
                heads = [rows_of(cols[t][q], r) for q in range(BLOCK)]
                for i in range(t, 8):
                    factor = cols[i][p] * inverse
                    if i == t:
                        factor = jnp.where(row > r, factor, 0.0)
                    s[i] = s[i] - factor * pivot_row
                    for q in range(p + 1, BLOCK):
                        cols[i][q] = cols[i][q] - factor * heads[q]
                pivots = jnp.where(row == r, pivot, pivots)
        out.append(s[t] * lax.rsqrt(pivots))
    return jnp.concatenate(out, axis=0)[:, 64:128]


def kernel(
    x_hbm, f2_hbm, f3_hbm, f4_hbm, b0_hbm, out_ref,
    xv, f2v, f3v, f4s, b0v, f2p, f2g, f3g, b0g, yh, ym, yl,
    s1, r1, vt, v_ref, a_ref, gp, g3, gsum, gfull, gmat, z_ref, linv_ref,
    loc, snd, rcv,
):
    w = lax.axis_index("wa")
    n = lax.axis_index("an")
    core = lax.rem(w, 2)
    chip = w // 2
    label = lax.rem(7 * chip, CHIPS)
    slot = label * 2 + core

    local = [
        pltpu.make_async_copy(f2_hbm, f2v, loc.at[0]),
        pltpu.make_async_copy(f3_hbm, f3v, loc.at[1]),
        pltpu.make_async_copy(b0_hbm, b0v, loc.at[2]),
        pltpu.make_async_copy(f4_hbm, f4s, loc.at[3]),
        pltpu.make_async_copy(x_hbm, xv, loc.at[4]),
    ]
    for copy in local:
        copy.start()

    barrier = pltpu.get_barrier_semaphore()

    def plane_peer(k):
        return lax.rem(w + k, NW), n

    def column_peer(k):
        return chip * 2 + lax.rem(core + k, 2), lax.rem(n + k // 2, NZ)

    @pl.loop(1, NW)
    def _(k):
        pl.semaphore_signal(barrier, inc=1, device_id=plane_peer(k), device_id_type=MESH)

    @pl.loop(2, 2 * NZ)
    def _(k):
        pl.semaphore_signal(barrier, inc=1, device_id=column_peer(k), device_id_type=MESH)

    local[0].wait()
    local[1].wait()
    local[2].wait()
    f2p[:, 0:64] = f2v[0:16, :]
    f2p[:, 64:128] = f2v[16:32, :]
    f2g[w] = f2p[...]
    f3g[n] = f3v[...]
    b0g[slot] = b0v[...]

    local[3].wait()
    local[4].wait()
    for bt in range(8):
        parts = [xv[pl.ds(bt * 4 + d, 128, stride=32), :] for d in range(4)]
        for g in range(2):
            total = parts[0] * f4s[g, 0]
            for d in range(1, 4):
                total = total + parts[d] * f4s[g, d]
            h, m, l = split3(total)
            here = (slice(128 * g, 128 * g + 128), slice(128 * bt, 128 * bt + 128))
            yh[here] = h
            ym[here] = m
            yl[here] = l

    pl.semaphore_wait(barrier, NW - 1 + 2 * NZ - 2)

    def send(stage, src, dst, peer):
        pltpu.make_async_remote_copy(
            src_ref=src, dst_ref=dst, send_sem=snd.at[stage], recv_sem=rcv.at[stage],
            device_id=peer, device_id_type=MESH,
        ).start()

    def await_all(sem, blocks):
        pltpu.make_async_copy(blocks, blocks, sem).wait()

    @pl.loop(1, NW)
    def _(k):
        send(0, f2p, f2g.at[w], plane_peer(k))

    @pl.loop(1, NZ)
    def _(k):
        send(1, f3v, f3g.at[n], (w, lax.rem(n + k, NZ)))

    await_all(rcv.at[0], f2g.at[pl.ds(0, NW - 1)])
    packed = f2g[...]
    full_two = jnp.concatenate([packed[:, :, 0:64], packed[:, :, 64:128]], axis=1)
    wh, wm, wl = split3(full_two.reshape(1024, 64))
    p0 = mm16(yh[...], jnp.concatenate([wh, wm, wl], axis=1))
    p1 = mm16(ym[...], jnp.concatenate([wh, wm], axis=1))
    p2 = mm16(yl[...], wh)
    first = (p0[:, 128:192] + p1[:, 64:128] + p2) + (p0[:, 64:128] + p1[:, 0:64]) + p0[:, 0:64]
    for g in range(2):
        s1[g] = first[128 * g : 128 * g + 128].T.reshape(8, 8, 128)

    @pl.loop(1, 2 * NZ)
    def _(k):
        to_w, to_n = column_peer(k)
        send(3, s1.at[lax.rem(to_w, 2), to_n], r1.at[core * NZ + n], (to_w, to_n))

    @pl.loop(1, NW)
    def _(k):
        send(2, b0v, b0g.at[slot], plane_peer(k))

    r1[core * NZ + n] = s1[core, n]
    await_all(rcv.at[1], f3g.at[pl.ds(0, NZ - 1)])
    full_three = f3g[...].reshape(128, 64)
    await_all(rcv.at[3], r1.at[pl.ds(0, 2 * NZ - 1)])

    lane = lax.broadcasted_iota(jnp.int32, (8, 128), 1)
    rows = []
    for s in range(2):
        v = [r1[s * NZ + m] for m in range(NZ)]
        for d in (4, 2, 1):
            upper = lax.rem(lane // (16 * d), 2) == 1
            nxt = list(v)
            for i in range(8):
                if i & d == 0:
                    j = i + d
                    nxt[i] = jnp.where(upper, pltpu.roll(v[j], 16 * d, 1), v[i])
                    nxt[j] = jnp.where(upper, v[j], pltpu.roll(v[i], 128 - 16 * d, 1))
            v = nxt
        rows += v
    vt[...] = mm(jnp.concatenate(rows, axis=0), full_three)
    for e in range(8):
        v_ref[:, 64 * e : 64 * e + 64] = vt[pl.ds(e, 16, stride=8), :]

    @pl.loop(1, HALF + 1)
    def _(k):
        to = lax.rem(7 * lax.rem(label + CHIPS - k, CHIPS), CHIPS)
        send(4, v_ref, a_ref.at[k], (to * 2 + core, n))

    a_ref[0] = v_ref[...]
    await_all(rcv.at[4], a_ref.at[pl.ds(1, HALF)])
    partial = mm(v_ref[...], a_ref[...].reshape(144, 512), ((1,), (1,)))
    row = lax.broadcasted_iota(jnp.int32, (8, 128), 0)
    for s in range(2):
        gp[s, 0:8] = partial[8 * s : 8 * s + 8, 0:128]
        last = jnp.concatenate([partial[8 * s : 8 * s + 8, 128:144]] * 8, axis=1)
        gp[s, 8:9] = jnp.sum(jnp.where(lane // 16 == lax.rem(8 - row, 8), last, 0.0), axis=0, keepdims=True)

    @pl.loop(1, 2 * NZ)
    def _(k):
        to_w, to_n = column_peer(k)
        send(
            5, gp.at[lax.rem(to_w, 2), pl.ds(0, 9)], g3.at[core * NZ + n, pl.ds(0, 9)], (to_w, to_n)
        )

    g3[core * NZ + n, 0:9] = gp[core, 0:9]
    await_all(rcv.at[5], g3.at[pl.ds(0, 2 * NZ - 1), pl.ds(0, 9)])
    for part in (slice(0, 8), slice(8, 9)):
        total = g3[0, part]
        for i in range(1, 2 * NZ):
            total = total + g3[i, part]
        gsum[part] = total * (1.0 / float(RANK * RANK * RANK_FOUR))

    @pl.loop(1, NW)
    def _(k):
        send(6, gsum.at[pl.ds(0, 9)], gfull.at[slot, pl.ds(0, 9)], plane_peer(k))

    gfull[slot, 0:9] = gsum[0:9]
    await_all(rcv.at[2], b0g.at[pl.ds(0, NW - 1)])
    basis = b0g[...].reshape(256, 64)
    await_all(rcv.at[6], gfull.at[pl.ds(0, NW - 1), pl.ds(0, 9)])

    for i in range(CHIPS):
        at = 16 * (i % 8)
        for c in range(2):
            body = gfull[2 * i + c, 0:8]
            if at:
                body = pltpu.roll(body, at, 1)
            last = jnp.broadcast_to(gfull[2 * i + c, 8:9], (8, 128))
            last = pltpu.roll(last, 0, 1, stride=16, stride_axis=0)
            if at:
                last = pltpu.roll(last, at, 1)
            near = jnp.where(lane >= at, body, 0.0)
            far = jnp.where(lane < at, body, jnp.where(lane < at + 16, last, 0.0))
            half = i // 8
            rows = slice(16 * i + 8 * c, 16 * i + 8 * c + 8)
            gmat[rows, 128 * half : 128 * half + 128] = near
            gmat[rows, 128 - 128 * half : 256 - 128 * half] = far
    half_gram = gmat[...]
    row_block = lax.broadcasted_iota(jnp.int32, (256, 256), 0) // 16
    column_block = lax.broadcasted_iota(jnp.int32, (256, 256), 1) // 16
    held = lax.rem(column_block - row_block + CHIPS, CHIPS) <= HALF
    gmat[...] = jnp.where(held, half_gram, half_gram.T)
    z_ref[...] = mm(gmat[...], basis)

    @pl.loop(0, ITERS)
    def _(step):
        z = z_ref[...]
        linv_ref[...] = inverse_cholesky(mm(z, z, ((0,), (0,))))

        @pl.when(step < ITERS - 1)
        def _():
            image = mm(gmat[...], z)
            z_ref[...] = mm(image, linv_ref[...], ((1,), (1,)))

    mine = z_ref[pl.ds(pl.multiple_of(slot * 8, 8), 8), :]
    out_ref[...] = mm(mine, linv_ref[...], ((1,), (1,))) * math.sqrt(256.0)

    await_all(snd.at[0], f2g.at[pl.ds(0, NW - 1)])
    await_all(snd.at[1], f3g.at[pl.ds(0, NZ - 1)])
    await_all(snd.at[2], b0g.at[pl.ds(0, NW - 1)])
    await_all(snd.at[3], r1.at[pl.ds(0, 2 * NZ - 1)])
    await_all(snd.at[4], a_ref.at[pl.ds(1, HALF)])
    await_all(snd.at[5], g3.at[pl.ds(0, 2 * NZ - 1), pl.ds(0, 9)])
    await_all(snd.at[6], gfull.at[pl.ds(0, NW - 1), pl.ds(0, 9)])


def per_device(tensor, factor_two, factor_three, factor_four, start_basis):
    f32, bf16 = jnp.float32, jnp.bfloat16
    x = tensor.reshape(8, 8, 128, 16, 4).transpose(0, 3, 1, 4, 2).reshape(4096, 128)
    hbm = pl.BlockSpec(memory_space=pltpu.HBM)
    return pl.pallas_call(
        kernel,
        out_shape=jax.ShapeDtypeStruct((8, 64), f32),
        in_specs=[hbm] * 5,
        out_specs=pl.BlockSpec(memory_space=pltpu.VMEM),
        scratch_shapes=[
            pltpu.VMEM((4096, 128), f32),
            pltpu.VMEM((32, 64), f32),
            pltpu.VMEM((16, 64), f32),
            pltpu.SMEM((2, 4), f32),
            pltpu.VMEM((8, 64), f32),
            pltpu.VMEM((16, 128), f32),
            pltpu.VMEM((NW, 16, 128), f32),
            pltpu.VMEM((NZ, 16, 64), f32),
            pltpu.VMEM((NW, 8, 64), f32),
            pltpu.VMEM((256, 1024), bf16),
            pltpu.VMEM((256, 1024), bf16),
            pltpu.VMEM((256, 1024), bf16),
            pltpu.VMEM((2, 8, 8, 128), f32),
            pltpu.VMEM((16, 8, 128), f32),
            pltpu.VMEM((128, 64), f32),
            pltpu.VMEM((16, 512), f32),
            pltpu.VMEM((HALF + 1, 16, 512), f32),
            pltpu.VMEM((2, 16, 128), f32),
            pltpu.VMEM((16, 16, 128), f32),
            pltpu.VMEM((16, 128), f32),
            pltpu.VMEM((NW, 16, 128), f32),
            pltpu.VMEM((256, 256), f32),
            pltpu.VMEM((256, 64), f32),
            pltpu.VMEM((64, 64), f32),
            pltpu.SemaphoreType.DMA((5,)),
            pltpu.SemaphoreType.DMA((7,)),
            pltpu.SemaphoreType.DMA((7,)),
        ],
        compiler_params=pltpu.CompilerParams(
            collective_id=0, has_side_effects=True, vmem_limit_bytes=60 * 2**20
        ),
        name="hooi",
    )(x, factor_two, factor_three, factor_four.T, start_basis)


def solution(mesh):
    in_specs = (P("wa", None, "an", None), P("wa", None), P("an", None), P(), P("wa", None))
    return jax.shard_map(
        per_device, mesh=mesh, in_specs=in_specs, out_specs=P("wa", None), check_vma=False
    )
```

```python
import functools
import math

import jax
import jax.numpy as jnp
from jax import lax
from jax.experimental import pallas as pl
from jax.experimental.pallas import tpu as pltpu
from jax.sharding import PartitionSpec as P

RANK = 64
RANK_FOUR = 2
ITERS = 4
NW, NZ = 32, 8
CHIPS = NW // 2
HALF = CHIPS // 2
BLOCK = 8
PLANE = sorted(
    [(x, y, c) for x in range(4) for y in range(4) for c in range(2) if x or y or c],
    key=lambda p: -(min(p[0], 4 - p[0]) + min(p[1], 4 - p[1])),
)
MESH = pl.DeviceIdType.MESH
HIGHEST = lax.Precision.HIGHEST


def split3(x):
    h = x.astype(jnp.bfloat16)
    rest = x - h.astype(jnp.float32)
    m = rest.astype(jnp.bfloat16)
    l = (rest - m.astype(jnp.float32)).astype(jnp.bfloat16)
    return h, m, l


def mm(a, b, dims=((1,), (0,))):
    return lax.dot_general(
        a, b, (dims, ((), ())), precision=HIGHEST, preferred_element_type=jnp.float32
    )


def mm16(a, b):
    return jnp.dot(a, b, preferred_element_type=jnp.float32)


def lanes_of(tile, column):
    return jnp.broadcast_to(tile[:, column : column + 1], (8, 128))


def rows_of(tile, row):
    return jnp.broadcast_to(tile[row : row + 1, :], (8, 128))


def inverse_cholesky(w):
    row = lax.broadcasted_iota(jnp.int32, (8, 128), 0)
    lane = lax.broadcasted_iota(jnp.int32, (8, 128), 1)
    wide = jnp.concatenate([w, jnp.zeros((64, 64), jnp.float32)], axis=1)
    s = []
    for i in range(8):
        unit = jnp.where(lane == row + (64 + 8 * i), 1.0, 0.0)
        s.append(jnp.where(lane < 64, wide[8 * i : 8 * i + 8], unit))
    out = []
    for t in range(8):
        pivots = jnp.ones((8, 128), jnp.float32)
        for start in range(0, 8, BLOCK):
            cols = {
                i: [lanes_of(s[i], 8 * t + start + q) for q in range(BLOCK)]
                for i in range(t, 8)
            }
            for p in range(BLOCK):
                r = start + p
                pivot_row = rows_of(s[t], r)
                pivot = rows_of(cols[t][p], r)
                inverse = 1.0 / pivot
                heads = [rows_of(cols[t][q], r) for q in range(BLOCK)]
                for i in range(t, 8):
                    factor = cols[i][p] * inverse
                    if i == t:
                        factor = jnp.where(row > r, factor, 0.0)
                    s[i] = s[i] - factor * pivot_row
                    for q in range(p + 1, BLOCK):
                        cols[i][q] = cols[i][q] - factor * heads[q]
                pivots = jnp.where(row == r, pivot, pivots)
        out.append(s[t] * lax.rsqrt(pivots))
    return jnp.concatenate(out, axis=0)[:, 64:128]


def kernel(
    x_hbm, f2_hbm, f3_hbm, f4_hbm, b0_hbm, out_ref,
    xv, f2v, f3v, f4s, b0v, f2p, f2g, f3g, b0g, yh, ym, yl,
    s1, r1, vt, v_ref, a_ref, gp, g3, gsum, gfull, gmat, z_ref, linv_ref,
    loc, snd, rcv,
):
    w = lax.axis_index("wa")
    n = lax.axis_index("an")
    core = lax.rem(w, 2)
    chip = w // 2
    label = lax.rem(7 * chip, CHIPS)
    slot = label * 2 + core

    local = [
        pltpu.make_async_copy(f2_hbm, f2v, loc.at[0]),
        pltpu.make_async_copy(f3_hbm, f3v, loc.at[1]),
        pltpu.make_async_copy(b0_hbm, b0v, loc.at[2]),
        pltpu.make_async_copy(f4_hbm, f4s, loc.at[3]),
        pltpu.make_async_copy(x_hbm, xv, loc.at[4]),
    ]
    for copy in local:
        copy.start()

    barrier = pltpu.get_barrier_semaphore()

    def plane_peers():
        for dx, dy, dc in PLANE:
            to = lax.rem(chip // 4 + dx, 4) * 4 + lax.rem(chip + dy, 4)
            yield to * 2 + lax.rem(core + dc, 2), n

    def column_peer(k):
        step = k // 2
        reach = (step + 1) // 2
        dz = NZ // 2 + reach * (1 - 2 * lax.rem(step, 2))
        return chip * 2 + lax.rem(core + k + 1, 2), lax.rem(n + dz, NZ)

    for peer in plane_peers():
        pl.semaphore_signal(barrier, inc=1, device_id=peer, device_id_type=MESH)

    @pl.loop(0, 2 * NZ - 2)
    def _(k):
        pl.semaphore_signal(barrier, inc=1, device_id=column_peer(k), device_id_type=MESH)

    local[0].wait()
    local[1].wait()
    local[2].wait()
    f2p[:, 0:64] = f2v[0:16, :]
    f2p[:, 64:128] = f2v[16:32, :]
    f2g[w] = f2p[...]
    f3g[n] = f3v[...]
    b0g[slot] = b0v[...]

    pl.semaphore_wait(barrier, NW - 1 + 2 * NZ - 2)

    def send(stage, src, dst, peer):
        pltpu.make_async_remote_copy(
            src_ref=src, dst_ref=dst, send_sem=snd.at[stage], recv_sem=rcv.at[stage],
            device_id=peer, device_id_type=MESH,
        ).start()

    def await_all(sem, blocks):
        pltpu.make_async_copy(blocks, blocks, sem).wait()

    for peer in plane_peers():
        send(0, f2p, f2g.at[w], peer)

    @pl.loop(1, NZ)
    def _(k):
        send(1, f3v, f3g.at[n], (w, lax.rem(n + k, NZ)))

    local[3].wait()
    local[4].wait()
    for bt in range(8):
        parts = [xv[pl.ds(bt * 4 + d, 128, stride=32), :] for d in range(4)]
        for g in range(2):
            total = parts[0] * f4s[g, 0]
            for d in range(1, 4):
                total = total + parts[d] * f4s[g, d]
            h, m, l = split3(total)
            here = (slice(128 * g, 128 * g + 128), slice(128 * bt, 128 * bt + 128))
            yh[here] = h
            ym[here] = m
            yl[here] = l

    await_all(rcv.at[0], f2g.at[pl.ds(0, NW - 1)])
    packed = f2g[...]
    full_two = jnp.concatenate([packed[:, :, 0:64], packed[:, :, 64:128]], axis=1)
    wh, wm, wl = split3(full_two.reshape(1024, 64))
    p0 = mm16(yh[...], jnp.concatenate([wh, wm, wl], axis=1))
    p1 = mm16(ym[...], jnp.concatenate([wh, wm], axis=1))
    p2 = mm16(yl[...], wh)
    first = (p0[:, 128:192] + p1[:, 64:128] + p2) + (p0[:, 64:128] + p1[:, 0:64]) + p0[:, 0:64]
    for g in range(2):
        s1[g] = first[128 * g : 128 * g + 128].T.reshape(8, 8, 128)

    @pl.loop(0, 2 * NZ - 1)
    def _(k):
        to_w, to_n = column_peer(k)
        send(3, s1.at[lax.rem(to_w, 2), to_n], r1.at[core * NZ + n], (to_w, to_n))

    for peer in plane_peers():
        send(2, b0v, b0g.at[slot], peer)

    r1[core * NZ + n] = s1[core, n]
    await_all(rcv.at[1], f3g.at[pl.ds(0, NZ - 1)])
    full_three = f3g[...].reshape(128, 64)
    await_all(rcv.at[3], r1.at[pl.ds(0, 2 * NZ - 1)])

    lane = lax.broadcasted_iota(jnp.int32, (8, 128), 1)
    rows = []
    for s in range(2):
        v = [r1[s * NZ + m] for m in range(NZ)]
        for d in (4, 2, 1):
            upper = lax.rem(lane // (16 * d), 2) == 1
            nxt = list(v)
            for i in range(8):
                if i & d == 0:
                    j = i + d
                    nxt[i] = jnp.where(upper, pltpu.roll(v[j], 16 * d, 1), v[i])
                    nxt[j] = jnp.where(upper, v[j], pltpu.roll(v[i], 128 - 16 * d, 1))
            v = nxt
        rows += v
    vt[...] = mm(jnp.concatenate(rows, axis=0), full_three)
    for e in range(8):
        v_ref[:, 64 * e : 64 * e + 64] = vt[pl.ds(e, 16, stride=8), :]

    @pl.loop(1, HALF + 1)
    def _(k):
        to = lax.rem(7 * lax.rem(label + CHIPS - k, CHIPS), CHIPS)
        send(4, v_ref, a_ref.at[k], (to * 2 + core, n))

    a_ref[0] = v_ref[...]
    await_all(rcv.at[4], a_ref.at[pl.ds(1, HALF)])
    partial = mm(v_ref[...], a_ref[...].reshape(144, 512), ((1,), (1,)))
    row = lax.broadcasted_iota(jnp.int32, (8, 128), 0)
    for s in range(2):
        gp[s, 0:8] = partial[8 * s : 8 * s + 8, 0:128]
        last = jnp.concatenate([partial[8 * s : 8 * s + 8, 128:144]] * 8, axis=1)
        gp[s, 8:9] = jnp.sum(jnp.where(lane // 16 == lax.rem(8 - row, 8), last, 0.0), axis=0, keepdims=True)

    @pl.loop(0, 2 * NZ - 1)
    def _(k):
        to_w, to_n = column_peer(k)
        send(
            5, gp.at[lax.rem(to_w, 2), pl.ds(0, 9)], g3.at[core * NZ + n, pl.ds(0, 9)], (to_w, to_n)
        )

    g3[core * NZ + n, 0:9] = gp[core, 0:9]
    await_all(rcv.at[5], g3.at[pl.ds(0, 2 * NZ - 1), pl.ds(0, 9)])
    for part in (slice(0, 8), slice(8, 9)):
        total = g3[0, part]
        for i in range(1, 2 * NZ):
            total = total + g3[i, part]
        gsum[part] = total * (1.0 / float(RANK * RANK * RANK_FOUR))

    for peer in plane_peers():
        send(6, gsum.at[pl.ds(0, 9)], gfull.at[slot, pl.ds(0, 9)], peer)

    gfull[slot, 0:9] = gsum[0:9]
    await_all(rcv.at[2], b0g.at[pl.ds(0, NW - 1)])
    basis = b0g[...].reshape(256, 64)
    await_all(rcv.at[6], gfull.at[pl.ds(0, NW - 1), pl.ds(0, 9)])

    for i in range(CHIPS):
        at = 16 * (i % 8)
        for c in range(2):
            body = gfull[2 * i + c, 0:8]
            if at:
                body = pltpu.roll(body, at, 1)
            last = jnp.broadcast_to(gfull[2 * i + c, 8:9], (8, 128))
            last = pltpu.roll(last, 0, 1, stride=16, stride_axis=0)
            if at:
                last = pltpu.roll(last, at, 1)
            near = jnp.where(lane >= at, body, 0.0)
            far = jnp.where(lane < at, body, jnp.where(lane < at + 16, last, 0.0))
            half = i // 8
            rows = slice(16 * i + 8 * c, 16 * i + 8 * c + 8)
            gmat[rows, 128 * half : 128 * half + 128] = near
            gmat[rows, 128 - 128 * half : 256 - 128 * half] = far
    half_gram = gmat[...]
    row_block = lax.broadcasted_iota(jnp.int32, (256, 256), 0) // 16
    column_block = lax.broadcasted_iota(jnp.int32, (256, 256), 1) // 16
    held = lax.rem(column_block - row_block + CHIPS, CHIPS) <= HALF
    gmat[...] = jnp.where(held, half_gram, half_gram.T)
    z_ref[...] = mm(gmat[...], basis)

    @pl.loop(0, ITERS)
    def _(step):
        z = z_ref[...]
        linv_ref[...] = inverse_cholesky(mm(z, z, ((0,), (0,))))

        @pl.when(step < ITERS - 1)
        def _():
            image = mm(gmat[...], z)
            z_ref[...] = mm(image, linv_ref[...], ((1,), (1,)))

    mine = z_ref[pl.ds(pl.multiple_of(slot * 8, 8), 8), :]
    out_ref[...] = mm(mine, linv_ref[...], ((1,), (1,))) * math.sqrt(256.0)

    await_all(snd.at[0], f2g.at[pl.ds(0, NW - 1)])
    await_all(snd.at[1], f3g.at[pl.ds(0, NZ - 1)])
    await_all(snd.at[2], b0g.at[pl.ds(0, NW - 1)])
    await_all(snd.at[3], r1.at[pl.ds(0, 2 * NZ - 1)])
    await_all(snd.at[4], a_ref.at[pl.ds(1, HALF)])
    await_all(snd.at[5], g3.at[pl.ds(0, 2 * NZ - 1), pl.ds(0, 9)])
    await_all(snd.at[6], gfull.at[pl.ds(0, NW - 1), pl.ds(0, 9)])


def per_device(tensor, factor_two, factor_three, factor_four, start_basis):
    f32, bf16 = jnp.float32, jnp.bfloat16
    x = tensor.reshape(8, 8, 128, 16, 4).transpose(0, 3, 1, 4, 2).reshape(4096, 128)
    hbm = pl.BlockSpec(memory_space=pltpu.HBM)
    return pl.pallas_call(
        kernel,
        out_shape=jax.ShapeDtypeStruct((8, 64), f32),
        in_specs=[hbm] * 5,
        out_specs=pl.BlockSpec(memory_space=pltpu.VMEM),
        scratch_shapes=[
            pltpu.VMEM((4096, 128), f32),
            pltpu.VMEM((32, 64), f32),
            pltpu.VMEM((16, 64), f32),
            pltpu.SMEM((2, 4), f32),
            pltpu.VMEM((8, 64), f32),
            pltpu.VMEM((16, 128), f32),
            pltpu.VMEM((NW, 16, 128), f32),
            pltpu.VMEM((NZ, 16, 64), f32),
            pltpu.VMEM((NW, 8, 64), f32),
            pltpu.VMEM((256, 1024), bf16),
            pltpu.VMEM((256, 1024), bf16),
            pltpu.VMEM((256, 1024), bf16),
            pltpu.VMEM((2, 8, 8, 128), f32),
            pltpu.VMEM((16, 8, 128), f32),
            pltpu.VMEM((128, 64), f32),
            pltpu.VMEM((16, 512), f32),
            pltpu.VMEM((HALF + 1, 16, 512), f32),
            pltpu.VMEM((2, 16, 128), f32),
            pltpu.VMEM((16, 16, 128), f32),
            pltpu.VMEM((16, 128), f32),
            pltpu.VMEM((NW, 16, 128), f32),
            pltpu.VMEM((256, 256), f32),
            pltpu.VMEM((256, 64), f32),
            pltpu.VMEM((64, 64), f32),
            pltpu.SemaphoreType.DMA((5,)),
            pltpu.SemaphoreType.DMA((7,)),
            pltpu.SemaphoreType.DMA((7,)),
        ],
        compiler_params=pltpu.CompilerParams(
            collective_id=0, has_side_effects=True, vmem_limit_bytes=60 * 2**20
        ),
        name="hooi",
    )(x, factor_two, factor_three, factor_four.T, start_basis)


def solution(mesh):
    in_specs = (P("wa", None, "an", None), P("wa", None), P("an", None), P(), P("wa", None))
    return jax.shard_map(
        per_device, mesh=mesh, in_specs=in_specs, out_specs=P("wa", None), check_vma=False
    )
```

```python
import functools
import math

import jax
import jax.numpy as jnp
from jax import lax
from jax.experimental import pallas as pl
from jax.experimental.pallas import tpu as pltpu
from jax.sharding import PartitionSpec as P

RANK = 64
RANK_FOUR = 2
ITERS = 4
NW, NZ = 32, 8
CHIPS = NW // 2
HALF = CHIPS // 2
PLANE = sorted(
    [(x, y, c) for x in range(4) for y in range(4) for c in range(2) if x or y or c],
    key=lambda p: -(min(p[0], 4 - p[0]) + min(p[1], 4 - p[1])),
)
MESH = pl.DeviceIdType.MESH
HIGHEST = lax.Precision.HIGHEST


def split3(x):
    h = x.astype(jnp.bfloat16)
    rest = x - h.astype(jnp.float32)
    m = rest.astype(jnp.bfloat16)
    l = (rest - m.astype(jnp.float32)).astype(jnp.bfloat16)
    return h, m, l


def mm(a, b, dims=((1,), (0,))):
    return lax.dot_general(
        a, b, (dims, ((), ())), precision=HIGHEST, preferred_element_type=jnp.float32
    )


def mm16(a, b):
    return jnp.dot(a, b, preferred_element_type=jnp.float32)


def mm_rows(a, b, dims):
    def parts(x, y):
        return lax.dot_general(x, y, (dims, ((), ())), preferred_element_type=jnp.float32)

    ah, am, al = split3(a)
    bh, bm, bl = split3(b)
    n = a.shape[0]
    high = parts(jnp.concatenate([ah, am, al], axis=0), bh)
    mid = parts(jnp.concatenate([ah, am], axis=0), bm)
    low = parts(ah, bl)
    return ((high[2 * n :] + low + mid[n:]) + (high[n : 2 * n] + mid[:n])) + high[:n]


def lanes_of(tile, column):
    return jnp.broadcast_to(tile[:, column : column + 1], (8, 128))


def rows_of(tile, row):
    return jnp.broadcast_to(tile[row : row + 1, :], (8, 128))


def inverse_cholesky(wide):
    row = lax.broadcasted_iota(jnp.int32, (8, 128), 0)
    lane = lax.broadcasted_iota(jnp.int32, (8, 128), 1)
    s = [
        wide[8 * i : 8 * i + 8] + jnp.where(lane == row + 8 * i, 1.0, 0.0) for i in range(8)
    ]
    out = []
    ahead = [lanes_of(s[0], 64 + q) for q in range(8)]
    for t in range(8):
        cols = {
            i: [lanes_of(s[i], 64 + 8 * t + q) for q in range(8)] for i in range(t + 1, 8)
        }
        cols[t] = ahead
        if t < 7:
            ahead = [lanes_of(s[t + 1], 64 + 8 * (t + 1) + q) for q in range(8)]
        pivots = jnp.ones((8, 128), jnp.float32)
        for p in range(8):
            pivot_row = rows_of(s[t], p)
            pivot = rows_of(cols[t][p], p)
            inverse = 1.0 / pivot
            heads = [rows_of(cols[t][q], p) for q in range(8)]
            for i in range(t, 8):
                factor = cols[i][p] * inverse
                if i == t:
                    factor = jnp.where(row > p, factor, 0.0)
                if i == t + 1:
                    for q in range(8):
                        ahead[q] = ahead[q] - factor * rows_of(cols[i][p], q)
                s[i] = s[i] - factor * pivot_row
                for q in range(p + 1, 8):
                    cols[i][q] = cols[i][q] - factor * heads[q]
            pivots = jnp.where(row == p, pivot, pivots)
        out.append(s[t] * lax.rsqrt(pivots))
    return jnp.concatenate(out, axis=0)[:, 0:64]


def kernel(
    x_hbm, f2_hbm, f3_hbm, f4_hbm, b0_hbm, out_ref,
    xv, f2v, f3v, f4s, b0v, f2p, f2g, f3g, b0g, yh, ym, yl,
    s1, r1, vt, v_ref, a_ref, gp, g3, gsum, gfull, gmat, zt_ref, z_ref, linv_ref,
    loc, snd, rcv,
):
    w = lax.axis_index("wa")
    n = lax.axis_index("an")
    core = lax.rem(w, 2)
    chip = w // 2
    label = lax.rem(7 * chip, CHIPS)
    slot = label * 2 + core

    local = [
        pltpu.make_async_copy(f2_hbm, f2v, loc.at[0]),
        pltpu.make_async_copy(f3_hbm, f3v, loc.at[1]),
        pltpu.make_async_copy(b0_hbm, b0v, loc.at[2]),
        pltpu.make_async_copy(f4_hbm, f4s, loc.at[3]),
        pltpu.make_async_copy(x_hbm, xv, loc.at[4]),
    ]
    for copy in local:
        copy.start()

    barrier = pltpu.get_barrier_semaphore()

    def plane_peers():
        for dx, dy, dc in PLANE:
            to = lax.rem(chip // 4 + dx, 4) * 4 + lax.rem(chip + dy, 4)
            yield to * 2 + lax.rem(core + dc, 2), n

    def column_peer(k):
        step = k // 2
        reach = (step + 1) // 2
        dz = NZ // 2 + reach * (1 - 2 * lax.rem(step, 2))
        return chip * 2 + lax.rem(core + k + 1, 2), lax.rem(n + dz, NZ)

    for peer in plane_peers():
        pl.semaphore_signal(barrier, inc=1, device_id=peer, device_id_type=MESH)

    @pl.loop(0, 2 * NZ - 2)
    def _(k):
        pl.semaphore_signal(barrier, inc=1, device_id=column_peer(k), device_id_type=MESH)

    local[0].wait()
    local[1].wait()
    local[2].wait()
    f2p[:, 0:64] = f2v[0:16, :]
    f2p[:, 64:128] = f2v[16:32, :]
    f2g[w] = f2p[...]
    f3g[n] = f3v[...]
    b0g[slot] = b0v[...]

    pl.semaphore_wait(barrier, NW - 1 + 2 * NZ - 2)

    def send(stage, src, dst, peer):
        pltpu.make_async_remote_copy(
            src_ref=src, dst_ref=dst, send_sem=snd.at[stage], recv_sem=rcv.at[stage],
            device_id=peer, device_id_type=MESH,
        ).start()

    def await_all(sem, blocks):
        pltpu.make_async_copy(blocks, blocks, sem).wait()

    for peer in plane_peers():
        send(0, f2p, f2g.at[w], peer)

    @pl.loop(1, NZ)
    def _(k):
        send(1, f3v, f3g.at[n], (w, lax.rem(n + k, NZ)))

    local[3].wait()
    local[4].wait()
    for bt in range(8):
        parts = [xv[pl.ds(bt * 4 + d, 128, stride=32), :] for d in range(4)]
        for g in range(2):
            total = parts[0] * f4s[g, 0]
            for d in range(1, 4):
                total = total + parts[d] * f4s[g, d]
            h, m, l = split3(total)
            here = (slice(128 * g, 128 * g + 128), slice(128 * bt, 128 * bt + 128))
            yh[here] = h
            ym[here] = m
            yl[here] = l

    await_all(rcv.at[0], f2g.at[pl.ds(0, NW - 1)])
    packed = f2g[...]
    full_two = jnp.concatenate([packed[:, :, 0:64], packed[:, :, 64:128]], axis=1)
    wh, wm, wl = split3(full_two.reshape(1024, 64))
    p0 = mm16(yh[...], jnp.concatenate([wh, wm, wl], axis=1))
    p1 = mm16(ym[...], jnp.concatenate([wh, wm], axis=1))
    p2 = mm16(yl[...], wh)
    first = (p0[:, 128:192] + p1[:, 64:128] + p2) + (p0[:, 64:128] + p1[:, 0:64]) + p0[:, 0:64]
    for g in range(2):
        s1[g] = first[128 * g : 128 * g + 128].T.reshape(8, 8, 128)

    @pl.loop(0, 2 * NZ - 1)
    def _(k):
        to_w, to_n = column_peer(k)
        send(3, s1.at[lax.rem(to_w, 2), to_n], r1.at[core * NZ + n], (to_w, to_n))

    for peer in plane_peers():
        send(2, b0v, b0g.at[slot], peer)

    r1[core * NZ + n] = s1[core, n]
    await_all(rcv.at[1], f3g.at[pl.ds(0, NZ - 1)])
    full_three = f3g[...].reshape(128, 64)
    await_all(rcv.at[3], r1.at[pl.ds(0, 2 * NZ - 1)])

    lane = lax.broadcasted_iota(jnp.int32, (8, 128), 1)
    rows = []
    for s in range(2):
        v = [r1[s * NZ + m] for m in range(NZ)]
        for d in (4, 2, 1):
            upper = lax.rem(lane // (16 * d), 2) == 1
            nxt = list(v)
            for i in range(8):
                if i & d == 0:
                    j = i + d
                    nxt[i] = jnp.where(upper, pltpu.roll(v[j], 16 * d, 1), v[i])
                    nxt[j] = jnp.where(upper, v[j], pltpu.roll(v[i], 128 - 16 * d, 1))
            v = nxt
        rows += v
    vt[...] = mm(jnp.concatenate(rows, axis=0), full_three)
    for e in range(8):
        v_ref[:, 64 * e : 64 * e + 64] = vt[pl.ds(e, 16, stride=8), :]

    @pl.loop(1, HALF + 1)
    def _(k):
        to = lax.rem(7 * lax.rem(label + CHIPS - k, CHIPS), CHIPS)
        send(4, v_ref, a_ref.at[k], (to * 2 + core, n))

    a_ref[0] = v_ref[...]
    await_all(rcv.at[4], a_ref.at[pl.ds(1, HALF)])
    partial = mm(v_ref[...], a_ref[...].reshape(144, 512), ((1,), (1,)))
    row = lax.broadcasted_iota(jnp.int32, (8, 128), 0)
    for s in range(2):
        gp[s, 0:8] = partial[8 * s : 8 * s + 8, 0:128]
        last = jnp.concatenate([partial[8 * s : 8 * s + 8, 128:144]] * 8, axis=1)
        gp[s, 8:9] = jnp.sum(jnp.where(lane // 16 == lax.rem(8 - row, 8), last, 0.0), axis=0, keepdims=True)

    @pl.loop(0, 2 * NZ - 1)
    def _(k):
        to_w, to_n = column_peer(k)
        send(
            5, gp.at[lax.rem(to_w, 2), pl.ds(0, 9)], g3.at[core * NZ + n, pl.ds(0, 9)], (to_w, to_n)
        )

    g3[core * NZ + n, 0:9] = gp[core, 0:9]
    await_all(rcv.at[5], g3.at[pl.ds(0, 2 * NZ - 1), pl.ds(0, 9)])
    for part in (slice(0, 8), slice(8, 9)):
        total = g3[0, part]
        for i in range(1, 2 * NZ):
            total = total + g3[i, part]
        gsum[part] = total * (1.0 / float(RANK * RANK * RANK_FOUR))

    for peer in plane_peers():
        send(6, gsum.at[pl.ds(0, 9)], gfull.at[slot, pl.ds(0, 9)], peer)

    gfull[slot, 0:9] = gsum[0:9]
    await_all(rcv.at[2], b0g.at[pl.ds(0, NW - 1)])
    basis_t = b0g[...].reshape(256, 64).T
    await_all(rcv.at[6], gfull.at[pl.ds(0, NW - 1), pl.ds(0, 9)])

    for i in range(CHIPS):
        at = 16 * (i % 8)
        for c in range(2):
            body = gfull[2 * i + c, 0:8]
            if at:
                body = pltpu.roll(body, at, 1)
            last = jnp.broadcast_to(gfull[2 * i + c, 8:9], (8, 128))
            last = pltpu.roll(last, 0, 1, stride=16, stride_axis=0)
            if at:
                last = pltpu.roll(last, at, 1)
            near = jnp.where(lane >= at, body, 0.0)
            far = jnp.where(lane < at, body, jnp.where(lane < at + 16, last, 0.0))
            half = i // 8
            rows = slice(16 * i + 8 * c, 16 * i + 8 * c + 8)
            gmat[rows, 128 * half : 128 * half + 128] = near
            gmat[rows, 128 - 128 * half : 256 - 128 * half] = far
    half_gram = gmat[...]
    row_block = lax.broadcasted_iota(jnp.int32, (256, 256), 0) // 16
    column_block = lax.broadcasted_iota(jnp.int32, (256, 256), 1) // 16
    held = lax.rem(column_block - row_block + CHIPS, CHIPS) <= HALF
    gmat[...] = jnp.where(held, half_gram, half_gram.T)
    zt_ref[...] = mm_rows(basis_t, gmat[...], ((1,), (0,)))

    @pl.loop(0, ITERS)
    def _(step):
        zt = zt_ref[...]
        below = jnp.concatenate([jnp.zeros((64, 256), jnp.float32), zt], axis=0)
        linv = inverse_cholesky(mm_rows(zt, below, ((1,), (1,))))
        linv_ref[...] = linv
        z_ref[...] = zt.T
        image_t = mm(zt, gmat[...])
        zt_ref[...] = mm_rows(linv, image_t, ((1,), (0,)))

    mine = z_ref[pl.ds(pl.multiple_of(slot * 8, 8), 8), :]
    out_ref[...] = mm(mine, linv_ref[...], ((1,), (1,))) * math.sqrt(256.0)

    await_all(snd.at[0], f2g.at[pl.ds(0, NW - 1)])
    await_all(snd.at[1], f3g.at[pl.ds(0, NZ - 1)])
    await_all(snd.at[2], b0g.at[pl.ds(0, NW - 1)])
    await_all(snd.at[3], r1.at[pl.ds(0, 2 * NZ - 1)])
    await_all(snd.at[4], a_ref.at[pl.ds(1, HALF)])
    await_all(snd.at[5], g3.at[pl.ds(0, 2 * NZ - 1), pl.ds(0, 9)])
    await_all(snd.at[6], gfull.at[pl.ds(0, NW - 1), pl.ds(0, 9)])


def per_device(tensor, factor_two, factor_three, factor_four, start_basis):
    f32, bf16 = jnp.float32, jnp.bfloat16
    x = tensor.reshape(8, 8, 128, 16, 4).transpose(0, 3, 1, 4, 2).reshape(4096, 128)
    hbm = pl.BlockSpec(memory_space=pltpu.HBM)
    return pl.pallas_call(
        kernel,
        out_shape=jax.ShapeDtypeStruct((8, 64), f32),
        in_specs=[hbm] * 5,
        out_specs=pl.BlockSpec(memory_space=pltpu.VMEM),
        scratch_shapes=[
            pltpu.VMEM((4096, 128), f32),
            pltpu.VMEM((32, 64), f32),
            pltpu.VMEM((16, 64), f32),
            pltpu.SMEM((2, 4), f32),
            pltpu.VMEM((8, 64), f32),
            pltpu.VMEM((16, 128), f32),
            pltpu.VMEM((NW, 16, 128), f32),
            pltpu.VMEM((NZ, 16, 64), f32),
            pltpu.VMEM((NW, 8, 64), f32),
            pltpu.VMEM((256, 1024), bf16),
            pltpu.VMEM((256, 1024), bf16),
            pltpu.VMEM((256, 1024), bf16),
            pltpu.VMEM((2, 8, 8, 128), f32),
            pltpu.VMEM((16, 8, 128), f32),
            pltpu.VMEM((128, 64), f32),
            pltpu.VMEM((16, 512), f32),
            pltpu.VMEM((HALF + 1, 16, 512), f32),
            pltpu.VMEM((2, 16, 128), f32),
            pltpu.VMEM((16, 16, 128), f32),
            pltpu.VMEM((16, 128), f32),
            pltpu.VMEM((NW, 16, 128), f32),
            pltpu.VMEM((256, 256), f32),
            pltpu.VMEM((64, 256), f32),
            pltpu.VMEM((256, 64), f32),
            pltpu.VMEM((64, 64), f32),
            pltpu.SemaphoreType.DMA((5,)),
            pltpu.SemaphoreType.DMA((7,)),
            pltpu.SemaphoreType.DMA((7,)),
        ],
        compiler_params=pltpu.CompilerParams(
            collective_id=0, has_side_effects=True, vmem_limit_bytes=60 * 2**20
        ),
        name="hooi",
    )(x, factor_two, factor_three, factor_four.T, start_basis)


def solution(mesh):
    in_specs = (P("wa", None, "an", None), P("wa", None), P("an", None), P(), P("wa", None))
    return jax.shard_map(
        per_device, mesh=mesh, in_specs=in_specs, out_specs=P("wa", None), check_vma=False
    )
```

```python
import functools
import math

import jax
import jax.numpy as jnp
from jax import lax
from jax.experimental import pallas as pl
from jax.experimental.pallas import tpu as pltpu
from jax.sharding import PartitionSpec as P

RANK = 64
RANK_FOUR = 2
ITERS = 4
NW, NZ = 32, 8
CHIPS = NW // 2
HALF = CHIPS // 2
def hops(peer):
    x, y, z, c = peer
    return min(x, 4 - x) + min(y, 4 - y) + min(z, NZ - z) + 0.5 * c


EVERY = sorted(
    [
        (x, y, z, c)
        for x in range(4)
        for y in range(4)
        for z in range(NZ)
        for c in range(2)
        if (x or y or z or c) and not ((x or y) and z)
    ],
    key=hops,
    reverse=True,
)
PLANE = [(x, y, c) for x, y, z, c in EVERY if z == 0]


MESH = pl.DeviceIdType.MESH
HIGHEST = lax.Precision.HIGHEST


def split3(x):
    h = x.astype(jnp.bfloat16)
    rest = x - h.astype(jnp.float32)
    m = rest.astype(jnp.bfloat16)
    l = (rest - m.astype(jnp.float32)).astype(jnp.bfloat16)
    return h, m, l


def mm(a, b, dims=((1,), (0,))):
    return lax.dot_general(
        a, b, (dims, ((), ())), precision=HIGHEST, preferred_element_type=jnp.float32
    )


def mm16(a, b):
    return jnp.dot(a, b, preferred_element_type=jnp.float32)


def mm_rows(a, b, dims):
    def parts(x, y):
        return lax.dot_general(x, y, (dims, ((), ())), preferred_element_type=jnp.float32)

    ah, am, al = split3(a)
    bh, bm, bl = split3(b)
    n = a.shape[0]
    high = parts(jnp.concatenate([ah, am, al], axis=0), bh)
    mid = parts(jnp.concatenate([ah, am], axis=0), bm)
    low = parts(ah, bl)
    return ((high[2 * n :] + low + mid[n:]) + (high[n : 2 * n] + mid[:n])) + high[:n]


def lanes_of(tile, column):
    return jnp.broadcast_to(tile[:, column : column + 1], (8, 128))


def rows_of(tile, row):
    return jnp.broadcast_to(tile[row : row + 1, :], (8, 128))


def inverse_cholesky(wide):
    row = lax.broadcasted_iota(jnp.int32, (8, 128), 0)
    lane = lax.broadcasted_iota(jnp.int32, (8, 128), 1)
    s = [
        wide[8 * i : 8 * i + 8] + jnp.where(lane == row + 8 * i, 1.0, 0.0) for i in range(8)
    ]
    out = []
    ahead = [lanes_of(s[0], 64 + q) for q in range(8)]
    for t in range(8):
        cols = {
            i: [lanes_of(s[i], 64 + 8 * t + q) for q in range(8)] for i in range(t + 1, 8)
        }
        cols[t] = ahead
        if t < 7:
            ahead = [lanes_of(s[t + 1], 64 + 8 * (t + 1) + q) for q in range(8)]
        pivots = jnp.ones((8, 128), jnp.float32)
        for p in range(8):
            pivot_row = rows_of(s[t], p)
            pivot = rows_of(cols[t][p], p)
            inverse = 1.0 / pivot
            heads = [rows_of(cols[t][q], p) for q in range(8)]
            for i in range(t, 8):
                factor = cols[i][p] * inverse
                if i == t:
                    factor = jnp.where(row > p, factor, 0.0)
                if i == t + 1:
                    for q in range(8):
                        ahead[q] = ahead[q] - factor * rows_of(cols[i][p], q)
                s[i] = s[i] - factor * pivot_row
                for q in range(p + 1, 8):
                    cols[i][q] = cols[i][q] - factor * heads[q]
            pivots = jnp.where(row == p, pivot, pivots)
        out.append(s[t] * lax.rsqrt(pivots))
    return jnp.concatenate(out, axis=0)[:, 0:64]


def kernel(
    x_hbm, f2_hbm, f3_hbm, f4_hbm, b0_hbm, out_ref,
    xv, f2v, f3v, f4s, b0v, f2p, f2g, f3g, b0g, yh, ym, yl,
    s1, r1, vt, v_ref, a_ref, gp, g3, gsum, gfull, gmat, zt_ref, z_ref, linv_ref,
    loc, snd, rcv,
):
    w = lax.axis_index("wa")
    n = lax.axis_index("an")
    core = lax.rem(w, 2)
    chip = w // 2
    label = lax.rem(7 * chip, CHIPS)
    slot = label * 2 + core

    local = [
        pltpu.make_async_copy(f2_hbm, f2v, loc.at[0]),
        pltpu.make_async_copy(f3_hbm, f3v, loc.at[1]),
        pltpu.make_async_copy(b0_hbm, b0v, loc.at[2]),
        pltpu.make_async_copy(f4_hbm, f4s, loc.at[3]),
        pltpu.make_async_copy(x_hbm, xv, loc.at[4]),
    ]
    for copy in local:
        copy.start()

    barrier = pltpu.get_barrier_semaphore()

    def plane_peers():
        for dx, dy, dc in PLANE:
            to = lax.rem(chip // 4 + dx, 4) * 4 + lax.rem(chip + dy, 4)
            yield to * 2 + lax.rem(core + dc, 2), n

    def column_peer(k):
        step = k // 2
        reach = (step + 1) // 2
        dz = NZ // 2 + reach * (1 - 2 * lax.rem(step, 2))
        return chip * 2 + lax.rem(core + k + 1, 2), lax.rem(n + dz, NZ)

    for dx, dy, dz, dc in EVERY:
        to = lax.rem(chip // 4 + dx, 4) * 4 + lax.rem(chip + dy, 4)
        peer = to * 2 + lax.rem(core + dc, 2), lax.rem(n + dz, NZ)
        pl.semaphore_signal(barrier, inc=1, device_id=peer, device_id_type=MESH)

    local[0].wait()
    local[1].wait()
    local[2].wait()
    f2p[:, 0:64] = f2v[0:16, :]
    f2p[:, 64:128] = f2v[16:32, :]
    f2g[w] = f2p[...]
    f3g[n] = f3v[...]
    b0g[slot] = b0v[...]

    pl.semaphore_wait(barrier, NW - 1 + 2 * NZ - 2)

    def send(stage, src, dst, peer):
        pltpu.make_async_remote_copy(
            src_ref=src, dst_ref=dst, send_sem=snd.at[stage], recv_sem=rcv.at[stage],
            device_id=peer, device_id_type=MESH,
        ).start()

    def await_all(sem, blocks):
        pltpu.make_async_copy(blocks, blocks, sem).wait()

    for peer in plane_peers():
        send(0, f2p, f2g.at[w], peer)

    @pl.loop(1, NZ)
    def _(k):
        send(1, f3v, f3g.at[n], (w, lax.rem(n + k, NZ)))

    local[3].wait()
    local[4].wait()
    for bt in range(8):
        parts = [xv[pl.ds(bt * 4 + d, 128, stride=32), :] for d in range(4)]
        for g in range(2):
            total = parts[0] * f4s[g, 0]
            for d in range(1, 4):
                total = total + parts[d] * f4s[g, d]
            h, m, l = split3(total)
            here = (slice(128 * g, 128 * g + 128), slice(128 * bt, 128 * bt + 128))
            yh[here] = h
            ym[here] = m
            yl[here] = l

    await_all(rcv.at[0], f2g.at[pl.ds(0, NW - 1)])
    packed = f2g[...]
    full_two = jnp.concatenate([packed[:, :, 0:64], packed[:, :, 64:128]], axis=1)
    wh, wm, wl = split3(full_two.reshape(1024, 64))
    p0 = mm16(yh[...], jnp.concatenate([wh, wm, wl], axis=1))
    p1 = mm16(ym[...], jnp.concatenate([wh, wm], axis=1))
    p2 = mm16(yl[...], wh)
    first = (p0[:, 128:192] + p1[:, 64:128] + p2) + (p0[:, 64:128] + p1[:, 0:64]) + p0[:, 0:64]
    for g in range(2):
        s1[g] = first[128 * g : 128 * g + 128].T.reshape(8, 8, 128)

    @pl.loop(0, 2 * NZ - 1)
    def _(k):
        to_w, to_n = column_peer(k)
        send(3, s1.at[lax.rem(to_w, 2), to_n], r1.at[core * NZ + n], (to_w, to_n))

    for peer in plane_peers():
        send(2, b0v, b0g.at[slot], peer)

    r1[core * NZ + n] = s1[core, n]
    await_all(rcv.at[1], f3g.at[pl.ds(0, NZ - 1)])
    full_three = f3g[...].reshape(128, 64)
    await_all(rcv.at[3], r1.at[pl.ds(0, 2 * NZ - 1)])

    lane = lax.broadcasted_iota(jnp.int32, (8, 128), 1)
    rows = []
    for s in range(2):
        v = [r1[s * NZ + m] for m in range(NZ)]
        for d in (4, 2, 1):
            upper = lax.rem(lane // (16 * d), 2) == 1
            nxt = list(v)
            for i in range(8):
                if i & d == 0:
                    j = i + d
                    nxt[i] = jnp.where(upper, pltpu.roll(v[j], 16 * d, 1), v[i])
                    nxt[j] = jnp.where(upper, v[j], pltpu.roll(v[i], 128 - 16 * d, 1))
            v = nxt
        rows += v
    vt[...] = mm(jnp.concatenate(rows, axis=0), full_three)
    for e in range(8):
        v_ref[:, 64 * e : 64 * e + 64] = vt[pl.ds(e, 16, stride=8), :]

    @pl.loop(1, HALF + 1)
    def _(k):
        to = lax.rem(7 * lax.rem(label + CHIPS - k, CHIPS), CHIPS)
        send(4, v_ref, a_ref.at[k], (to * 2 + core, n))

    a_ref[0] = v_ref[...]
    await_all(rcv.at[4], a_ref.at[pl.ds(1, HALF)])
    partial = mm_rows(v_ref[...], a_ref[...].reshape(144, 512), ((1,), (1,)))
    row = lax.broadcasted_iota(jnp.int32, (8, 128), 0)
    for s in range(2):
        gp[s, 0:8] = partial[8 * s : 8 * s + 8, 0:128]
        last = jnp.concatenate([partial[8 * s : 8 * s + 8, 128:144]] * 8, axis=1)
        gp[s, 8:9] = jnp.sum(jnp.where(lane // 16 == lax.rem(8 - row, 8), last, 0.0), axis=0, keepdims=True)

    @pl.loop(0, 2 * NZ - 1)
    def _(k):
        to_w, to_n = column_peer(k)
        send(
            5, gp.at[lax.rem(to_w, 2), pl.ds(0, 9)], g3.at[core * NZ + n, pl.ds(0, 9)], (to_w, to_n)
        )

    g3[core * NZ + n, 0:9] = gp[core, 0:9]
    await_all(rcv.at[5], g3.at[pl.ds(0, 2 * NZ - 1), pl.ds(0, 9)])
    for part in (slice(0, 8), slice(8, 9)):
        total = g3[0, part]
        for i in range(1, 2 * NZ):
            total = total + g3[i, part]
        gsum[part] = total * (1.0 / float(RANK * RANK * RANK_FOUR))

    for peer in plane_peers():
        send(6, gsum.at[pl.ds(0, 9)], gfull.at[slot, pl.ds(0, 9)], peer)

    gfull[slot, 0:9] = gsum[0:9]
    await_all(rcv.at[2], b0g.at[pl.ds(0, NW - 1)])
    basis_t = b0g[...].reshape(256, 64).T
    await_all(rcv.at[6], gfull.at[pl.ds(0, NW - 1), pl.ds(0, 9)])

    for i in range(CHIPS):
        at = 16 * (i % 8)
        for c in range(2):
            body = gfull[2 * i + c, 0:8]
            if at:
                body = pltpu.roll(body, at, 1)
            last = jnp.broadcast_to(gfull[2 * i + c, 8:9], (8, 128))
            last = pltpu.roll(last, 0, 1, stride=16, stride_axis=0)
            if at:
                last = pltpu.roll(last, at, 1)
            near = jnp.where(lane >= at, body, 0.0)
            far = jnp.where(lane < at, body, jnp.where(lane < at + 16, last, 0.0))
            half = i // 8
            rows = slice(16 * i + 8 * c, 16 * i + 8 * c + 8)
            gmat[rows, 128 * half : 128 * half + 128] = near
            gmat[rows, 128 - 128 * half : 256 - 128 * half] = far
    half_gram = gmat[...]
    row_block = lax.broadcasted_iota(jnp.int32, (256, 256), 0) // 16
    column_block = lax.broadcasted_iota(jnp.int32, (256, 256), 1) // 16
    held = lax.rem(column_block - row_block + CHIPS, CHIPS) <= HALF
    gmat[...] = jnp.where(held, half_gram, half_gram.T)
    zt_ref[...] = mm_rows(basis_t, gmat[...], ((1,), (0,)))

    @pl.loop(0, ITERS)
    def _(step):
        zt = zt_ref[...]
        below = jnp.concatenate([jnp.zeros((64, 256), jnp.float32), zt], axis=0)
        linv = inverse_cholesky(mm_rows(zt, below, ((1,), (1,))))
        linv_ref[...] = linv
        z_ref[...] = zt.T
        image_t = mm(zt, gmat[...])

        @pl.when(step < ITERS - 1)
        def _():
            zt_ref[...] = mm_rows(linv, image_t, ((1,), (0,)))

    mine = z_ref[pl.ds(pl.multiple_of(slot * 8, 8), 8), :]
    out_ref[...] = mm(mine, linv_ref[...], ((1,), (1,))) * math.sqrt(256.0)

    await_all(snd.at[0], f2g.at[pl.ds(0, NW - 1)])
    await_all(snd.at[1], f3g.at[pl.ds(0, NZ - 1)])
    await_all(snd.at[2], b0g.at[pl.ds(0, NW - 1)])
    await_all(snd.at[3], r1.at[pl.ds(0, 2 * NZ - 1)])
    await_all(snd.at[4], a_ref.at[pl.ds(1, HALF)])
    await_all(snd.at[5], g3.at[pl.ds(0, 2 * NZ - 1), pl.ds(0, 9)])
    await_all(snd.at[6], gfull.at[pl.ds(0, NW - 1), pl.ds(0, 9)])


def per_device(tensor, factor_two, factor_three, factor_four, start_basis):
    f32, bf16 = jnp.float32, jnp.bfloat16
    x = tensor.reshape(8, 8, 128, 16, 4).transpose(0, 3, 1, 4, 2).reshape(4096, 128)
    hbm = pl.BlockSpec(memory_space=pltpu.HBM)
    operands = (x, factor_two, factor_three, factor_four.T, start_basis)
    return pl.pallas_call(
        kernel,
        out_shape=jax.ShapeDtypeStruct((8, 64), f32),
        in_specs=[hbm] * 5,
        out_specs=pl.BlockSpec(memory_space=pltpu.VMEM),
        scratch_shapes=[
            pltpu.VMEM((4096, 128), f32),
            pltpu.VMEM((32, 64), f32),
            pltpu.VMEM((16, 64), f32),
            pltpu.SMEM((2, 4), f32),
            pltpu.VMEM((8, 64), f32),
            pltpu.VMEM((16, 128), f32),
            pltpu.VMEM((NW, 16, 128), f32),
            pltpu.VMEM((NZ, 16, 64), f32),
            pltpu.VMEM((NW, 8, 64), f32),
            pltpu.VMEM((256, 1024), bf16),
            pltpu.VMEM((256, 1024), bf16),
            pltpu.VMEM((256, 1024), bf16),
            pltpu.VMEM((2, 8, 8, 128), f32),
            pltpu.VMEM((16, 8, 128), f32),
            pltpu.VMEM((128, 64), f32),
            pltpu.VMEM((16, 512), f32),
            pltpu.VMEM((HALF + 1, 16, 512), f32),
            pltpu.VMEM((2, 16, 128), f32),
            pltpu.VMEM((16, 16, 128), f32),
            pltpu.VMEM((16, 128), f32),
            pltpu.VMEM((NW, 16, 128), f32),
            pltpu.VMEM((256, 256), f32),
            pltpu.VMEM((64, 256), f32),
            pltpu.VMEM((256, 64), f32),
            pltpu.VMEM((64, 64), f32),
            pltpu.SemaphoreType.DMA((5,)),
            pltpu.SemaphoreType.DMA((7,)),
            pltpu.SemaphoreType.DMA((7,)),
        ],
        compiler_params=pltpu.CompilerParams(
            collective_id=0, has_side_effects=True, vmem_limit_bytes=40 * 2**20
        ),
        name="hooi",
    )(*(pltpu.with_memory_space_constraint(v, pltpu.HBM) for v in operands))


def solution(mesh):
    in_specs = (P("wa", None, "an", None), P("wa", None), P("an", None), P(), P("wa", None))
    return jax.shard_map(
        per_device, mesh=mesh, in_specs=in_specs, out_specs=P("wa", None), check_vma=False
    )
```

```python
import functools
import math

import jax
import jax.numpy as jnp
from jax import lax
from jax.experimental import pallas as pl
from jax.experimental.pallas import tpu as pltpu
from jax.sharding import PartitionSpec as P

RANK = 64
RANK_FOUR = 2
ITERS = 4
NW, NZ = 32, 8
CHIPS = NW // 2
HALF = CHIPS // 2
def hops(peer):
    x, y, z, c = peer
    return min(x, 4 - x) + min(y, 4 - y) + min(z, NZ - z) + 0.5 * c


EVERY = sorted(
    [
        (x, y, z, c)
        for x in range(4)
        for y in range(4)
        for z in range(NZ)
        for c in range(2)
        if (x or y or z or c) and not ((x or y) and z)
    ],
    key=hops,
    reverse=True,
)
PLANE = [(x, y, c) for x, y, z, c in EVERY if z == 0]
COLUMN = [(z, c) for x, y, z, c in EVERY if x == 0 and y == 0]


MESH = pl.DeviceIdType.MESH
HIGHEST = lax.Precision.HIGHEST


def split3(x):
    h = x.astype(jnp.bfloat16)
    rest = x - h.astype(jnp.float32)
    m = rest.astype(jnp.bfloat16)
    l = (rest - m.astype(jnp.float32)).astype(jnp.bfloat16)
    return h, m, l


def mm(a, b, dims=((1,), (0,))):
    return lax.dot_general(
        a, b, (dims, ((), ())), precision=HIGHEST, preferred_element_type=jnp.float32
    )


def mm16(a, b):
    return jnp.dot(a, b, preferred_element_type=jnp.float32)


def mm_rows(a, b, dims):
    def parts(x, y):
        return lax.dot_general(x, y, (dims, ((), ())), preferred_element_type=jnp.float32)

    ah, am, al = split3(a)
    bh, bm, bl = split3(b)
    n = a.shape[0]
    high = parts(jnp.concatenate([ah, am, al], axis=0), bh)
    mid = parts(jnp.concatenate([ah, am], axis=0), bm)
    low = parts(ah, bl)
    return ((high[2 * n :] + low + mid[n:]) + (high[n : 2 * n] + mid[:n])) + high[:n]


def lanes_of(tile, column):
    return jnp.broadcast_to(tile[:, column : column + 1], (8, 128))


def rows_of(tile, row):
    return jnp.broadcast_to(tile[row : row + 1, :], (8, 128))


def inverse_cholesky(wide):
    row = lax.broadcasted_iota(jnp.int32, (8, 128), 0)
    lane = lax.broadcasted_iota(jnp.int32, (8, 128), 1)
    s = [
        wide[8 * i : 8 * i + 8] + jnp.where(lane == row + 8 * i, 1.0, 0.0) for i in range(8)
    ]
    out = []
    ahead = [lanes_of(s[0], 64 + q) for q in range(8)]
    for t in range(8):
        cols = {
            i: [lanes_of(s[i], 64 + 8 * t + q) for q in range(8)] for i in range(t + 1, 8)
        }
        cols[t] = ahead
        if t < 7:
            ahead = [lanes_of(s[t + 1], 64 + 8 * (t + 1) + q) for q in range(8)]
        pivots = jnp.ones((8, 128), jnp.float32)
        for p in range(8):
            pivot_row = rows_of(s[t], p)
            pivot = rows_of(cols[t][p], p)
            inverse = 1.0 / pivot
            heads = [rows_of(cols[t][q], p) for q in range(8)]
            for i in range(t, 8):
                factor = cols[i][p] * inverse
                if i == t:
                    factor = jnp.where(row > p, factor, 0.0)
                if i == t + 1:
                    for q in range(8):
                        ahead[q] = ahead[q] - factor * rows_of(cols[i][p], q)
                s[i] = s[i] - factor * pivot_row
                for q in range(p + 1, 8):
                    cols[i][q] = cols[i][q] - factor * heads[q]
            pivots = jnp.where(row == p, pivot, pivots)
        out.append(s[t] * lax.rsqrt(pivots))
    return jnp.concatenate(out, axis=0)[:, 0:64]


def kernel(
    x_hbm, f2_hbm, f3_hbm, f4_hbm, b0_hbm, out_ref,
    xv, f2v, f3v, f4s, b0v, f2p, f2g, f3g, b0g, yh, ym, yl,
    s1, r1, vt, v_ref, a_ref, gp, g3, gsum, gfull, gmat, zt_ref, z_ref, linv_ref,
    loc, snd, rcv,
):
    w = lax.axis_index("wa")
    n = lax.axis_index("an")
    core = lax.rem(w, 2)
    chip = w // 2
    label = lax.rem(7 * chip, CHIPS)
    slot = label * 2 + core

    local = [
        pltpu.make_async_copy(f2_hbm, f2v, loc.at[0]),
        pltpu.make_async_copy(f3_hbm, f3v, loc.at[1]),
        pltpu.make_async_copy(b0_hbm, b0v, loc.at[2]),
        pltpu.make_async_copy(f4_hbm, f4s, loc.at[3]),
        pltpu.make_async_copy(x_hbm, xv, loc.at[4]),
    ]
    for copy in local:
        copy.start()

    barrier = pltpu.get_barrier_semaphore()

    def plane_peers():
        for dx, dy, dc in PLANE:
            to = lax.rem(chip // 4 + dx, 4) * 4 + lax.rem(chip + dy, 4)
            yield to * 2 + lax.rem(core + dc, 2), n

    def column_peers():
        for dz, dc in COLUMN:
            to = lax.rem(core + dc, 2)
            yield to, (chip * 2 + to, lax.rem(n + dz, NZ))

    for dx, dy, dz, dc in EVERY:
        to = lax.rem(chip // 4 + dx, 4) * 4 + lax.rem(chip + dy, 4)
        peer = to * 2 + lax.rem(core + dc, 2), lax.rem(n + dz, NZ)
        pl.semaphore_signal(barrier, inc=1, device_id=peer, device_id_type=MESH)

    local[0].wait()
    local[1].wait()
    local[2].wait()
    f2p[:, 0:64] = f2v[0:16, :]
    f2p[:, 64:128] = f2v[16:32, :]
    f2g[w] = f2p[...]
    f3g[n] = f3v[...]
    b0g[slot] = b0v[...]

    pl.semaphore_wait(barrier, NW - 1 + 2 * NZ - 2)

    def send(stage, src, dst, peer):
        pltpu.make_async_remote_copy(
            src_ref=src, dst_ref=dst, send_sem=snd.at[stage], recv_sem=rcv.at[stage],
            device_id=peer, device_id_type=MESH,
        ).start()

    def await_all(sem, blocks):
        pltpu.make_async_copy(blocks, blocks, sem).wait()

    for peer in plane_peers():
        send(0, f2p, f2g.at[w], peer)

    @pl.loop(1, NZ)
    def _(k):
        send(1, f3v, f3g.at[n], (w, lax.rem(n + k, NZ)))

    local[3].wait()
    local[4].wait()
    for bt in range(8):
        parts = [xv[pl.ds(bt * 4 + d, 128, stride=32), :] for d in range(4)]
        for g in range(2):
            total = parts[0] * f4s[g, 0]
            for d in range(1, 4):
                total = total + parts[d] * f4s[g, d]
            h, m, l = split3(total)
            here = (slice(128 * g, 128 * g + 128), slice(128 * bt, 128 * bt + 128))
            yh[here] = h
            ym[here] = m
            yl[here] = l

    await_all(rcv.at[0], f2g.at[pl.ds(0, NW - 1)])
    wh, wm, wl = (
        jnp.concatenate([v[:, :, 0:64], v[:, :, 64:128]], axis=1).reshape(1024, 64)
        for v in split3(f2g[...])
    )
    p0 = mm16(yh[...], jnp.concatenate([wh, wm, wl], axis=1))
    p1 = mm16(ym[...], jnp.concatenate([wh, wm], axis=1))
    p2 = mm16(yl[...], wh)
    first = (p0[:, 128:192] + p1[:, 64:128] + p2) + (p0[:, 64:128] + p1[:, 0:64]) + p0[:, 0:64]
    for g in range(2):
        s1[g] = first[128 * g : 128 * g + 128].T.reshape(8, 8, 128)

    for to, peer in column_peers():
        send(3, s1.at[to, peer[1]], r1.at[core * NZ + n], peer)

    for peer in plane_peers():
        send(2, b0v, b0g.at[slot], peer)

    r1[core * NZ + n] = s1[core, n]
    await_all(rcv.at[1], f3g.at[pl.ds(0, NZ - 1)])
    full_three = f3g[...].reshape(128, 64)
    await_all(rcv.at[3], r1.at[pl.ds(0, 2 * NZ - 1)])

    lane = lax.broadcasted_iota(jnp.int32, (8, 128), 1)
    rows = []
    for s in range(2):
        v = [r1[s * NZ + m] for m in range(NZ)]
        for d in (4, 2, 1):
            upper = lax.rem(lane // (16 * d), 2) == 1
            nxt = list(v)
            for i in range(8):
                if i & d == 0:
                    j = i + d
                    nxt[i] = jnp.where(upper, pltpu.roll(v[j], 16 * d, 1), v[i])
                    nxt[j] = jnp.where(upper, v[j], pltpu.roll(v[i], 128 - 16 * d, 1))
            v = nxt
        rows += v
    vt[...] = mm(jnp.concatenate(rows, axis=0), full_three)
    for e in range(8):
        v_ref[:, 64 * e : 64 * e + 64] = vt[pl.ds(e, 16, stride=8), :]

    for k in (1, 3, 6, 2, 5, 7, 8, 4):
        to = lax.rem(7 * lax.rem(label + CHIPS - k, CHIPS), CHIPS)
        send(4, v_ref, a_ref.at[k], (to * 2 + core, n))

    a_ref[0] = v_ref[...]
    await_all(rcv.at[4], a_ref.at[pl.ds(1, HALF)])
    partial = mm_rows(v_ref[...], a_ref[...].reshape(144, 512), ((1,), (1,)))
    row = lax.broadcasted_iota(jnp.int32, (8, 128), 0)
    for s in range(2):
        gp[s, 0:8] = partial[8 * s : 8 * s + 8, 0:128]
        last = jnp.concatenate([partial[8 * s : 8 * s + 8, 128:144]] * 8, axis=1)
        gp[s, 8:9] = jnp.sum(jnp.where(lane // 16 == lax.rem(8 - row, 8), last, 0.0), axis=0, keepdims=True)

    for to, peer in column_peers():
        send(5, gp.at[to, pl.ds(0, 9)], g3.at[core * NZ + n, pl.ds(0, 9)], peer)

    g3[core * NZ + n, 0:9] = gp[core, 0:9]
    await_all(rcv.at[5], g3.at[pl.ds(0, 2 * NZ - 1), pl.ds(0, 9)])
    for part in (slice(0, 8), slice(8, 9)):
        total = g3[0, part]
        for i in range(1, 2 * NZ):
            total = total + g3[i, part]
        gsum[part] = total * (1.0 / float(RANK * RANK * RANK_FOUR))

    for peer in plane_peers():
        send(6, gsum.at[pl.ds(0, 9)], gfull.at[slot, pl.ds(0, 9)], peer)

    gfull[slot, 0:9] = gsum[0:9]
    await_all(rcv.at[2], b0g.at[pl.ds(0, NW - 1)])
    basis_t = b0g[...].reshape(256, 64).T
    await_all(rcv.at[6], gfull.at[pl.ds(0, NW - 1), pl.ds(0, 9)])

    for i in range(CHIPS):
        at = 16 * (i % 8)
        for c in range(2):
            body = gfull[2 * i + c, 0:8]
            if at:
                body = pltpu.roll(body, at, 1)
            last = jnp.broadcast_to(gfull[2 * i + c, 8:9], (8, 128))
            last = pltpu.roll(last, 0, 1, stride=16, stride_axis=0)
            if at:
                last = pltpu.roll(last, at, 1)
            near = jnp.where(lane >= at, body, 0.0)
            far = jnp.where(lane < at, body, jnp.where(lane < at + 16, last, 0.0))
            half = i // 8
            rows = slice(16 * i + 8 * c, 16 * i + 8 * c + 8)
            gmat[rows, 128 * half : 128 * half + 128] = near
            gmat[rows, 128 - 128 * half : 256 - 128 * half] = far
    half_gram = gmat[...]
    row_block = lax.broadcasted_iota(jnp.int32, (256, 256), 0) // 16
    column_block = lax.broadcasted_iota(jnp.int32, (256, 256), 1) // 16
    held = lax.rem(column_block - row_block + CHIPS, CHIPS) <= HALF
    gmat[...] = jnp.where(held, half_gram, half_gram.T)
    zt_ref[...] = mm_rows(basis_t, gmat[...], ((1,), (0,)))

    @pl.loop(0, ITERS)
    def _(step):
        zt = zt_ref[...]
        below = jnp.concatenate([jnp.zeros((64, 256), jnp.float32), zt], axis=0)
        linv = inverse_cholesky(mm_rows(zt, below, ((1,), (1,))))
        linv_ref[...] = linv
        image_t = mm(zt, gmat[...])

        @pl.when(step < ITERS - 1)
        def _():
            zt_ref[...] = mm_rows(linv, image_t, ((1,), (0,)))

    z_ref[...] = zt_ref[...].T
    mine = z_ref[pl.ds(pl.multiple_of(slot * 8, 8), 8), :]
    out_ref[...] = mm(mine, linv_ref[...], ((1,), (1,))) * math.sqrt(256.0)

    await_all(snd.at[0], f2g.at[pl.ds(0, NW - 1)])
    await_all(snd.at[1], f3g.at[pl.ds(0, NZ - 1)])
    await_all(snd.at[2], b0g.at[pl.ds(0, NW - 1)])
    await_all(snd.at[3], r1.at[pl.ds(0, 2 * NZ - 1)])
    await_all(snd.at[4], a_ref.at[pl.ds(1, HALF)])
    await_all(snd.at[5], g3.at[pl.ds(0, 2 * NZ - 1), pl.ds(0, 9)])
    await_all(snd.at[6], gfull.at[pl.ds(0, NW - 1), pl.ds(0, 9)])


def per_device(tensor, factor_two, factor_three, factor_four, start_basis):
    f32, bf16 = jnp.float32, jnp.bfloat16
    x = tensor.reshape(8, 8, 128, 16, 4).transpose(0, 3, 1, 4, 2).reshape(4096, 128)
    hbm = pl.BlockSpec(memory_space=pltpu.HBM)
    operands = (x, factor_two, factor_three, factor_four.T, start_basis)
    return pl.pallas_call(
        kernel,
        out_shape=jax.ShapeDtypeStruct((8, 64), f32),
        in_specs=[hbm] * 5,
        out_specs=pl.BlockSpec(memory_space=pltpu.VMEM),
        scratch_shapes=[
            pltpu.VMEM((4096, 128), f32),
            pltpu.VMEM((32, 64), f32),
            pltpu.VMEM((16, 64), f32),
            pltpu.SMEM((2, 4), f32),
            pltpu.VMEM((8, 64), f32),
            pltpu.VMEM((16, 128), f32),
            pltpu.VMEM((NW, 16, 128), f32),
            pltpu.VMEM((NZ, 16, 64), f32),
            pltpu.VMEM((NW, 8, 64), f32),
            pltpu.VMEM((256, 1024), bf16),
            pltpu.VMEM((256, 1024), bf16),
            pltpu.VMEM((256, 1024), bf16),
            pltpu.VMEM((2, 8, 8, 128), f32),
            pltpu.VMEM((16, 8, 128), f32),
            pltpu.VMEM((128, 64), f32),
            pltpu.VMEM((16, 512), f32),
            pltpu.VMEM((HALF + 1, 16, 512), f32),
            pltpu.VMEM((2, 16, 128), f32),
            pltpu.VMEM((16, 16, 128), f32),
            pltpu.VMEM((16, 128), f32),
            pltpu.VMEM((NW, 16, 128), f32),
            pltpu.VMEM((256, 256), f32),
            pltpu.VMEM((64, 256), f32),
            pltpu.VMEM((256, 64), f32),
            pltpu.VMEM((64, 64), f32),
            pltpu.SemaphoreType.DMA((5,)),
            pltpu.SemaphoreType.DMA((7,)),
            pltpu.SemaphoreType.DMA((7,)),
        ],
        compiler_params=pltpu.CompilerParams(
            collective_id=0, has_side_effects=True, vmem_limit_bytes=40 * 2**20
        ),
        name="hooi",
    )(*(pltpu.with_memory_space_constraint(v, pltpu.HBM) for v in operands))


def solution(mesh):
    in_specs = (P("wa", None, "an", None), P("wa", None), P("an", None), P(), P("wa", None))
    return jax.shard_map(
        per_device, mesh=mesh, in_specs=in_specs, out_specs=P("wa", None), check_vma=False
    )
```

```python
import functools
import math

import jax
import jax.numpy as jnp
from jax import lax
from jax.experimental import pallas as pl
from jax.experimental.pallas import tpu as pltpu
from jax.sharding import PartitionSpec as P

RANK = 64
RANK_FOUR = 2
ITERS = 4
NW, NZ = 32, 8
CHIPS = NW // 2
HALF = CHIPS // 2
def hops(peer):
    x, y, z, c = peer
    return min(x, 4 - x) + min(y, 4 - y) + min(z, NZ - z) + 0.5 * c


EVERY = sorted(
    [
        (x, y, z, c)
        for x in range(4)
        for y in range(4)
        for z in range(NZ)
        for c in range(2)
        if (x or y or z or c) and not ((x or y) and z)
    ],
    key=hops,
    reverse=True,
)
PLANE = [(x, y, c) for x, y, z, c in EVERY if z == 0]
COLUMN = [(z, c) for x, y, z, c in EVERY if x == 0 and y == 0]


MESH = pl.DeviceIdType.MESH
HIGHEST = lax.Precision.HIGHEST


def split3(x):
    h = x.astype(jnp.bfloat16)
    rest = x - h.astype(jnp.float32)
    m = rest.astype(jnp.bfloat16)
    l = (rest - m.astype(jnp.float32)).astype(jnp.bfloat16)
    return h, m, l


def mm(a, b, dims=((1,), (0,))):
    return lax.dot_general(
        a, b, (dims, ((), ())), precision=HIGHEST, preferred_element_type=jnp.float32
    )


def mm16(a, b):
    return jnp.dot(a, b, preferred_element_type=jnp.float32)


def mm_parts(a, b, dims):
    def product(x, y):
        return lax.dot_general(x, y, (dims, ((), ())), preferred_element_type=jnp.float32)

    ah, am, al = a
    bh, bm, bl = b
    n = ah.shape[0]
    high = product(jnp.concatenate([ah, am, al], axis=0), bh)
    mid = product(jnp.concatenate([ah, am], axis=0), bm)
    low = product(ah, bl)
    return ((high[2 * n :] + low + mid[n:]) + (high[n : 2 * n] + mid[:n])) + high[:n]


def mm_rows(a, b, dims):
    return mm_parts(split3(a), split3(b), dims)


def lanes_of(tile, column):
    return jnp.broadcast_to(tile[:, column : column + 1], (8, 128))


def rows_of(tile, row):
    return jnp.broadcast_to(tile[row : row + 1, :], (8, 128))


def inverse_cholesky(wide):
    row = lax.broadcasted_iota(jnp.int32, (8, 128), 0)
    lane = lax.broadcasted_iota(jnp.int32, (8, 128), 1)
    s = [
        wide[8 * i : 8 * i + 8] + jnp.where(lane == row + 8 * i, 1.0, 0.0) for i in range(8)
    ]
    out = []
    ahead = [lanes_of(s[0], 64 + q) for q in range(8)]
    for t in range(8):
        cols = {
            i: [lanes_of(s[i], 64 + 8 * t + q) for q in range(8)] for i in range(t + 1, 8)
        }
        cols[t] = ahead
        if t < 7:
            ahead = [lanes_of(s[t + 1], 64 + 8 * (t + 1) + q) for q in range(8)]
        pivots = jnp.ones((8, 128), jnp.float32)
        for p in range(8):
            pivot_row = rows_of(s[t], p)
            pivot = rows_of(cols[t][p], p)
            inverse = 1.0 / pivot
            heads = [rows_of(cols[t][q], p) for q in range(8)]
            for i in range(t, 8):
                factor = cols[i][p] * inverse
                if i == t:
                    factor = jnp.where(row > p, factor, 0.0)
                if i == t + 1:
                    for q in range(8):
                        ahead[q] = ahead[q] - factor * rows_of(cols[i][p], q)
                s[i] = s[i] - factor * pivot_row
                for q in range(p + 1, 8):
                    cols[i][q] = cols[i][q] - factor * heads[q]
            pivots = jnp.where(row == p, pivot, pivots)
        out.append(s[t] * lax.rsqrt(pivots))
    return jnp.concatenate(out, axis=0)[:, 0:64]


def kernel(
    x_hbm, f2_hbm, f3_hbm, f4_hbm, b0_hbm, out_ref,
    xv, f2v, f3v, f4s, b0v, f2p, f2g, f3g, b0g, yh, ym, yl,
    s1, r1, vt, v_ref, a_ref, gp, g3, gsum, gfull, gmat, gparts, zt_ref, z_ref, linv_ref,
    loc, snd, rcv,
):
    w = lax.axis_index("wa")
    n = lax.axis_index("an")
    core = lax.rem(w, 2)
    chip = w // 2
    label = lax.rem(7 * chip, CHIPS)
    slot = label * 2 + core

    local = [
        pltpu.make_async_copy(f2_hbm, f2v, loc.at[0]),
        pltpu.make_async_copy(f3_hbm, f3v, loc.at[1]),
        pltpu.make_async_copy(b0_hbm, b0v, loc.at[2]),
        pltpu.make_async_copy(f4_hbm, f4s, loc.at[3]),
        pltpu.make_async_copy(x_hbm, xv, loc.at[4]),
    ]
    local[0].start()

    barrier = pltpu.get_barrier_semaphore()

    def plane_peers():
        for dx, dy, dc in PLANE:
            to = lax.rem(chip // 4 + dx, 4) * 4 + lax.rem(chip + dy, 4)
            yield to * 2 + lax.rem(core + dc, 2), n

    def column_peers():
        for dz, dc in COLUMN:
            to = lax.rem(core + dc, 2)
            yield to, (chip * 2 + to, lax.rem(n + dz, NZ))

    for dx, dy, dz, dc in EVERY:
        to = lax.rem(chip // 4 + dx, 4) * 4 + lax.rem(chip + dy, 4)
        peer = to * 2 + lax.rem(core + dc, 2), lax.rem(n + dz, NZ)
        pl.semaphore_signal(barrier, inc=1, device_id=peer, device_id_type=MESH)

    for copy in local[1:]:
        copy.start()
    local[0].wait()
    local[1].wait()
    local[2].wait()
    f2p[:, 0:64] = f2v[0:16, :]
    f2p[:, 64:128] = f2v[16:32, :]
    f2g[w] = f2p[...]
    f3g[n] = f3v[...]
    b0g[slot] = b0v[...]

    pl.semaphore_wait(barrier, NW - 1 + 2 * NZ - 2)

    def send(stage, src, dst, peer):
        pltpu.make_async_remote_copy(
            src_ref=src, dst_ref=dst, send_sem=snd.at[stage], recv_sem=rcv.at[stage],
            device_id=peer, device_id_type=MESH,
        ).start()

    def await_all(sem, blocks):
        pltpu.make_async_copy(blocks, blocks, sem).wait()

    for peer in plane_peers():
        send(0, f2p, f2g.at[w], peer)

    @pl.loop(1, NZ)
    def _(k):
        send(1, f3v, f3g.at[n], (w, lax.rem(n + k, NZ)))

    local[3].wait()
    local[4].wait()
    for bt in range(8):
        parts = [xv[pl.ds(bt * 4 + d, 128, stride=32), :] for d in range(4)]
        for g in range(2):
            total = parts[0] * f4s[g, 0]
            for d in range(1, 4):
                total = total + parts[d] * f4s[g, d]
            h, m, l = split3(total)
            here = (slice(128 * g, 128 * g + 128), slice(128 * bt, 128 * bt + 128))
            yh[here] = h
            ym[here] = m
            yl[here] = l

    await_all(rcv.at[0], f2g.at[pl.ds(0, NW - 1)])
    wh, wm, wl = (
        jnp.concatenate([v[:, :, 0:64], v[:, :, 64:128]], axis=1).reshape(1024, 64)
        for v in split3(f2g[...])
    )
    p0 = mm16(yh[...], jnp.concatenate([wh, wm, wl], axis=1))
    p1 = mm16(ym[...], jnp.concatenate([wh, wm], axis=1))
    p2 = mm16(yl[...], wh)
    first = (p0[:, 128:192] + p1[:, 64:128] + p2) + (p0[:, 64:128] + p1[:, 0:64]) + p0[:, 0:64]
    for g in range(2):
        s1[g] = first[128 * g : 128 * g + 128].T.reshape(8, 8, 128)

    for to, peer in column_peers():
        send(3, s1.at[to, peer[1]], r1.at[core * NZ + n], peer)

    for peer in plane_peers():
        send(2, b0v, b0g.at[slot], peer)

    r1[core * NZ + n] = s1[core, n]
    await_all(rcv.at[1], f3g.at[pl.ds(0, NZ - 1)])
    full_three = f3g[...].reshape(128, 64)
    await_all(rcv.at[3], r1.at[pl.ds(0, 2 * NZ - 1)])

    lane = lax.broadcasted_iota(jnp.int32, (8, 128), 1)
    rows = []
    for s in range(2):
        v = [r1[s * NZ + m] for m in range(NZ)]
        for d in (4, 2, 1):
            upper = lax.rem(lane // (16 * d), 2) == 1
            nxt = list(v)
            for i in range(8):
                if i & d == 0:
                    j = i + d
                    nxt[i] = jnp.where(upper, pltpu.roll(v[j], 16 * d, 1), v[i])
                    nxt[j] = jnp.where(upper, v[j], pltpu.roll(v[i], 128 - 16 * d, 1))
            v = nxt
        rows += v
    vt[...] = mm(jnp.concatenate(rows, axis=0), full_three)
    for e in range(8):
        v_ref[:, 64 * e : 64 * e + 64] = vt[pl.ds(e, 16, stride=8), :]

    for k in (1, 3, 6, 2, 5, 7, 8, 4):
        to = lax.rem(7 * lax.rem(label + CHIPS - k, CHIPS), CHIPS)
        send(4, v_ref, a_ref.at[k], (to * 2 + core, n))

    a_ref[0] = v_ref[...]
    await_all(rcv.at[4], a_ref.at[pl.ds(1, HALF)])
    partial = mm_rows(v_ref[...], a_ref[...].reshape(144, 512), ((1,), (1,)))
    row = lax.broadcasted_iota(jnp.int32, (8, 128), 0)
    for s in range(2):
        gp[s, 0:8] = partial[8 * s : 8 * s + 8, 0:128]
        last = jnp.concatenate([partial[8 * s : 8 * s + 8, 128:144]] * 8, axis=1)
        gp[s, 8:9] = jnp.sum(jnp.where(lane // 16 == lax.rem(8 - row, 8), last, 0.0), axis=0, keepdims=True)

    for to, peer in column_peers():
        send(5, gp.at[to, pl.ds(0, 9)], g3.at[core * NZ + n, pl.ds(0, 9)], peer)

    g3[core * NZ + n, 0:9] = gp[core, 0:9]
    await_all(rcv.at[5], g3.at[pl.ds(0, 2 * NZ - 1), pl.ds(0, 9)])
    for part in (slice(0, 8), slice(8, 9)):
        total = g3[0, part]
        for i in range(1, 2 * NZ):
            total = total + g3[i, part]
        gsum[part] = total * (1.0 / float(RANK * RANK * RANK_FOUR))

    for peer in plane_peers():
        send(6, gsum.at[pl.ds(0, 9)], gfull.at[slot, pl.ds(0, 9)], peer)

    gfull[slot, 0:9] = gsum[0:9]
    await_all(rcv.at[2], b0g.at[pl.ds(0, NW - 1)])
    basis_t = b0g[...].reshape(256, 64).T
    await_all(rcv.at[6], gfull.at[pl.ds(0, NW - 1), pl.ds(0, 9)])

    for i in range(CHIPS):
        at = 16 * (i % 8)
        for c in range(2):
            body = gfull[2 * i + c, 0:8]
            if at:
                body = pltpu.roll(body, at, 1)
            last = jnp.broadcast_to(gfull[2 * i + c, 8:9], (8, 128))
            last = pltpu.roll(last, 0, 1, stride=16, stride_axis=0)
            if at:
                last = pltpu.roll(last, at, 1)
            near = jnp.where(lane >= at, body, 0.0)
            far = jnp.where(lane < at, body, jnp.where(lane < at + 16, last, 0.0))
            half = i // 8
            rows = slice(16 * i + 8 * c, 16 * i + 8 * c + 8)
            gmat[rows, 128 * half : 128 * half + 128] = near
            gmat[rows, 128 - 128 * half : 256 - 128 * half] = far
    half_gram = gmat[...]
    row_block = lax.broadcasted_iota(jnp.int32, (256, 256), 0) // 16
    column_block = lax.broadcasted_iota(jnp.int32, (256, 256), 1) // 16
    held = lax.rem(column_block - row_block + CHIPS, CHIPS) <= HALF
    gram = split3(jnp.where(held, half_gram, half_gram.T))
    for i in range(3):
        gparts[i] = gram[i]
    zt_ref[...] = mm_parts(split3(basis_t), gram, ((1,), (0,)))

    @pl.loop(0, ITERS)
    def _(step):
        zt = zt_ref[...]
        z = split3(zt)
        below = [jnp.concatenate([jnp.zeros((64, 256), v.dtype), v], axis=0) for v in z]
        linv = inverse_cholesky(mm_parts(z, below, ((1,), (1,))))
        linv_ref[...] = linv
        image_t = mm_parts(z, [gparts[i] for i in range(3)], ((1,), (0,)))

        @pl.when(step < ITERS - 1)
        def _():
            zt_ref[...] = mm_rows(linv, image_t, ((1,), (0,)))

    z_ref[...] = zt_ref[...].T
    mine = z_ref[pl.ds(pl.multiple_of(slot * 8, 8), 8), :]
    out_ref[...] = mm(mine, linv_ref[...], ((1,), (1,))) * math.sqrt(256.0)

    await_all(snd.at[0], f2g.at[pl.ds(0, NW - 1)])
    await_all(snd.at[1], f3g.at[pl.ds(0, NZ - 1)])
    await_all(snd.at[2], b0g.at[pl.ds(0, NW - 1)])
    await_all(snd.at[3], r1.at[pl.ds(0, 2 * NZ - 1)])
    await_all(snd.at[4], a_ref.at[pl.ds(1, HALF)])
    await_all(snd.at[5], g3.at[pl.ds(0, 2 * NZ - 1), pl.ds(0, 9)])
    await_all(snd.at[6], gfull.at[pl.ds(0, NW - 1), pl.ds(0, 9)])


def per_device(tensor, factor_two, factor_three, factor_four, start_basis):
    f32, bf16 = jnp.float32, jnp.bfloat16
    x = tensor.reshape(8, 8, 128, 16, 4).transpose(0, 3, 1, 4, 2).reshape(4096, 128)
    hbm = pl.BlockSpec(memory_space=pltpu.HBM)
    operands = (x, factor_two, factor_three, factor_four.T, start_basis)
    return pl.pallas_call(
        kernel,
        out_shape=jax.ShapeDtypeStruct((8, 64), f32),
        in_specs=[hbm] * 5,
        out_specs=pl.BlockSpec(memory_space=pltpu.VMEM),
        scratch_shapes=[
            pltpu.VMEM((4096, 128), f32),
            pltpu.VMEM((32, 64), f32),
            pltpu.VMEM((16, 64), f32),
            pltpu.SMEM((2, 4), f32),
            pltpu.VMEM((8, 64), f32),
            pltpu.VMEM((16, 128), f32),
            pltpu.VMEM((NW, 16, 128), f32),
            pltpu.VMEM((NZ, 16, 64), f32),
            pltpu.VMEM((NW, 8, 64), f32),
            pltpu.VMEM((256, 1024), bf16),
            pltpu.VMEM((256, 1024), bf16),
            pltpu.VMEM((256, 1024), bf16),
            pltpu.VMEM((2, 8, 8, 128), f32),
            pltpu.VMEM((16, 8, 128), f32),
            pltpu.VMEM((128, 64), f32),
            pltpu.VMEM((16, 512), f32),
            pltpu.VMEM((HALF + 1, 16, 512), f32),
            pltpu.VMEM((2, 16, 128), f32),
            pltpu.VMEM((16, 16, 128), f32),
            pltpu.VMEM((16, 128), f32),
            pltpu.VMEM((NW, 16, 128), f32),
            pltpu.VMEM((256, 256), f32),
            pltpu.VMEM((3, 256, 256), bf16),
            pltpu.VMEM((64, 256), f32),
            pltpu.VMEM((256, 64), f32),
            pltpu.VMEM((64, 64), f32),
            pltpu.SemaphoreType.DMA((5,)),
            pltpu.SemaphoreType.DMA((7,)),
            pltpu.SemaphoreType.DMA((7,)),
        ],
        compiler_params=pltpu.CompilerParams(
            collective_id=0, has_side_effects=True, vmem_limit_bytes=40 * 2**20
        ),
        name="hooi",
    )(*(pltpu.with_memory_space_constraint(v, pltpu.HBM) for v in operands))


def solution(mesh):
    in_specs = (P("wa", None, "an", None), P("wa", None), P("an", None), P(), P("wa", None))
    return jax.shard_map(
        per_device, mesh=mesh, in_specs=in_specs, out_specs=P("wa", None), check_vma=False
    )
```

```python
import functools
import math

import jax
import jax.numpy as jnp
from jax import lax
from jax.experimental import pallas as pl
from jax.experimental.pallas import tpu as pltpu
from jax.sharding import PartitionSpec as P

RANK = 64
RANK_FOUR = 2
ITERS = 4
NW, NZ = 32, 8
CHIPS = NW // 2
HALF = CHIPS // 2
def hops(peer):
    x, y, z, c = peer
    return min(x, 4 - x) + min(y, 4 - y) + min(z, NZ - z) + 0.5 * c


EVERY = sorted(
    [
        (x, y, z, c)
        for x in range(4)
        for y in range(4)
        for z in range(NZ)
        for c in range(2)
        if (x or y or z or c) and not ((x or y) and z)
    ],
    key=hops,
    reverse=True,
)
PLANE = [(x, y, c) for x, y, z, c in EVERY if z == 0]
COLUMN = [(z, c) for x, y, z, c in EVERY if x == 0 and y == 0]


MESH = pl.DeviceIdType.MESH
HIGHEST = lax.Precision.HIGHEST


def split3(x):
    h = x.astype(jnp.bfloat16)
    rest = x - h.astype(jnp.float32)
    m = rest.astype(jnp.bfloat16)
    l = (rest - m.astype(jnp.float32)).astype(jnp.bfloat16)
    return h, m, l


def mm(a, b, dims=((1,), (0,))):
    return lax.dot_general(
        a, b, (dims, ((), ())), precision=HIGHEST, preferred_element_type=jnp.float32
    )


def mm16(a, b):
    return jnp.dot(a, b, preferred_element_type=jnp.float32)


def mm_parts(a, b, dims):
    def product(x, y):
        return lax.dot_general(x, y, (dims, ((), ())), preferred_element_type=jnp.float32)

    ah, am, al = a
    bh, bm, bl = b
    n = ah.shape[0]
    high = product(jnp.concatenate([ah, am, al], axis=0), bh)
    mid = product(jnp.concatenate([ah, am], axis=0), bm)
    low = product(ah, bl)
    return ((high[2 * n :] + low + mid[n:]) + (high[n : 2 * n] + mid[:n])) + high[:n]


def mm_rows(a, b, dims):
    return mm_parts(split3(a), split3(b), dims)


def lanes_of(tile, column):
    return jnp.broadcast_to(tile[:, column : column + 1], (8, 128))


def rows_of(tile, row):
    return jnp.broadcast_to(tile[row : row + 1, :], (8, 128))


def inverse_cholesky(wide):
    row = lax.broadcasted_iota(jnp.int32, (8, 128), 0)
    lane = lax.broadcasted_iota(jnp.int32, (8, 128), 1)
    s = [
        wide[8 * i : 8 * i + 8] + jnp.where(lane == row + 8 * i, 1.0, 0.0) for i in range(8)
    ]
    out = []
    ahead = [lanes_of(s[0], 64 + q) for q in range(8)]
    for t in range(8):
        cols = {
            i: [lanes_of(s[i], 64 + 8 * t + q) for q in range(8)] for i in range(t + 1, 8)
        }
        cols[t] = ahead
        if t < 7:
            ahead = [lanes_of(s[t + 1], 64 + 8 * (t + 1) + q) for q in range(8)]
        pivots = jnp.ones((8, 128), jnp.float32)
        for p in range(8):
            pivot_row = rows_of(s[t], p)
            pivot = rows_of(cols[t][p], p)
            inverse = 1.0 / pivot
            heads = [rows_of(cols[t][q], p) for q in range(8)]
            for i in range(t, 8):
                factor = cols[i][p] * inverse
                if i == t:
                    factor = jnp.where(row > p, factor, 0.0)
                if i == t + 1:
                    for q in range(8):
                        ahead[q] = ahead[q] - factor * rows_of(cols[i][p], q)
                s[i] = s[i] - factor * pivot_row
                for q in range(p + 1, 8):
                    cols[i][q] = cols[i][q] - factor * heads[q]
            pivots = jnp.where(row == p, pivot, pivots)
        out.append(s[t] * lax.rsqrt(pivots))
    return jnp.concatenate(out, axis=0)[:, 0:64]


def kernel(
    x_hbm, f2_hbm, f3_hbm, f4_hbm, b0_hbm, out_ref,
    xv, f2v, f3v, f4s, b0v, f2p, f2g, f3g, b0g, yh, ym, yl,
    s1, r1, vt, v_ref, a_ref, gp, g3, gsum, gfull, gmat, gparts, zt_ref, z_ref, linv_ref,
    loc, snd, rcv,
):
    w = lax.axis_index("wa")
    n = lax.axis_index("an")
    core = lax.rem(w, 2)
    chip = w // 2
    label = lax.rem(7 * chip, CHIPS)
    slot = label * 2 + core

    local = [
        pltpu.make_async_copy(f2_hbm, f2v, loc.at[0]),
        pltpu.make_async_copy(f3_hbm, f3v, loc.at[1]),
        pltpu.make_async_copy(b0_hbm, b0v, loc.at[2]),
        pltpu.make_async_copy(f4_hbm, f4s, loc.at[3]),
        pltpu.make_async_copy(x_hbm, xv, loc.at[4]),
    ]
    local[0].start()

    barrier = pltpu.get_barrier_semaphore()

    def plane_peers():
        for dx, dy, dc in PLANE:
            to = lax.rem(chip // 4 + dx, 4) * 4 + lax.rem(chip + dy, 4)
            yield to * 2 + lax.rem(core + dc, 2), n

    def column_peers():
        for dz, dc in COLUMN:
            to = lax.rem(core + dc, 2)
            yield to, (chip * 2 + to, lax.rem(n + dz, NZ))

    for dx, dy, dz, dc in EVERY:
        to = lax.rem(chip // 4 + dx, 4) * 4 + lax.rem(chip + dy, 4)
        peer = to * 2 + lax.rem(core + dc, 2), lax.rem(n + dz, NZ)
        pl.semaphore_signal(barrier, inc=1, device_id=peer, device_id_type=MESH)

    for copy in local[1:]:
        copy.start()
    local[0].wait()
    local[1].wait()
    local[2].wait()
    f2p[:, 0:64] = f2v[0:16, :]
    f2p[:, 64:128] = f2v[16:32, :]
    f2g[core * CHIPS + chip] = f2p[...]
    f3g[n] = f3v[...]
    b0g[slot] = b0v[...]

    pl.semaphore_wait(barrier, NW - 1 + 2 * NZ - 2)

    def send(stage, src, dst, peer):
        pltpu.make_async_remote_copy(
            src_ref=src, dst_ref=dst, send_sem=snd.at[stage], recv_sem=rcv.at[stage],
            device_id=peer, device_id_type=MESH,
        ).start()

    def await_all(sem, blocks):
        pltpu.make_async_copy(blocks, blocks, sem).wait()

    for to, peer in zip(PLANE, plane_peers()):
        if to[2] == 0:
            send(0, f2p, f2g.at[core * CHIPS + chip], peer)

    @pl.loop(1, NZ)
    def _(k):
        send(1, f3v, f3g.at[n], (w, lax.rem(n + k, NZ)))

    local[3].wait()
    local[4].wait()
    for bt in range(8):
        parts = [xv[pl.ds(bt * 4 + d, 128, stride=32), :] for d in range(4)]
        for g in range(2):
            total = parts[0] * f4s[g, 0]
            for d in range(1, 4):
                total = total + parts[d] * f4s[g, d]
            h, m, l = split3(total)
            here = (slice(128 * g, 128 * g + 128), slice(128 * bt, 128 * bt + 128))
            yh[here] = h
            ym[here] = m
            yl[here] = l

    await_all(rcv.at[0], f2g.at[pl.ds(0, CHIPS - 1)])
    mine = f2g.at[pl.ds(core * CHIPS, CHIPS)]
    send(7, mine, mine, (chip * 2 + 1 - core, n))
    await_all(rcv.at[7], f2g.at[pl.ds(0, CHIPS)])
    halves = [split3(f2g[CHIPS * c : CHIPS * c + CHIPS]) for c in range(2)]
    wh, wm, wl = (
        jnp.concatenate(
            [v[:, :, 64 * h : 64 * h + 64] for v in pair for h in range(2)], axis=1
        ).reshape(1024, 64)
        for pair in zip(*halves)
    )
    p0 = mm16(yh[...], jnp.concatenate([wh, wm, wl], axis=1))
    p1 = mm16(ym[...], jnp.concatenate([wh, wm], axis=1))
    p2 = mm16(yl[...], wh)
    first = (p0[:, 128:192] + p1[:, 64:128] + p2) + (p0[:, 64:128] + p1[:, 0:64]) + p0[:, 0:64]
    for g in range(2):
        s1[g] = first[128 * g : 128 * g + 128].T.reshape(8, 8, 128)

    for to, peer in column_peers():
        send(3, s1.at[to, peer[1]], r1.at[core * NZ + n], peer)

    for peer in plane_peers():
        send(2, b0v, b0g.at[slot], peer)

    r1[core * NZ + n] = s1[core, n]
    await_all(rcv.at[1], f3g.at[pl.ds(0, NZ - 1)])
    full_three = f3g[...].reshape(128, 64)
    await_all(rcv.at[3], r1.at[pl.ds(0, 2 * NZ - 1)])

    lane = lax.broadcasted_iota(jnp.int32, (8, 128), 1)
    rows = []
    for s in range(2):
        v = [r1[s * NZ + m] for m in range(NZ)]
        for d in (4, 2, 1):
            upper = lax.rem(lane // (16 * d), 2) == 1
            nxt = list(v)
            for i in range(8):
                if i & d == 0:
                    j = i + d
                    nxt[i] = jnp.where(upper, pltpu.roll(v[j], 16 * d, 1), v[i])
                    nxt[j] = jnp.where(upper, v[j], pltpu.roll(v[i], 128 - 16 * d, 1))
            v = nxt
        rows += v
    vt[...] = mm(jnp.concatenate(rows, axis=0), full_three)
    for e in range(8):
        v_ref[:, 64 * e : 64 * e + 64] = vt[pl.ds(e, 16, stride=8), :]

    for k in (1, 3, 6, 2, 5, 7, 8, 4):
        to = lax.rem(7 * lax.rem(label + CHIPS - k, CHIPS), CHIPS)
        send(4, v_ref, a_ref.at[k], (to * 2 + core, n))

    a_ref[0] = v_ref[...]
    await_all(rcv.at[4], a_ref.at[pl.ds(1, HALF)])
    partial = mm_rows(v_ref[...], a_ref[...].reshape(144, 512), ((1,), (1,)))
    row = lax.broadcasted_iota(jnp.int32, (8, 128), 0)
    for s in range(2):
        gp[s, 0:8] = partial[8 * s : 8 * s + 8, 0:128]
        last = jnp.concatenate([partial[8 * s : 8 * s + 8, 128:144]] * 8, axis=1)
        gp[s, 8:9] = jnp.sum(jnp.where(lane // 16 == lax.rem(8 - row, 8), last, 0.0), axis=0, keepdims=True)

    for to, peer in column_peers():
        send(5, gp.at[to, pl.ds(0, 9)], g3.at[core * NZ + n, pl.ds(0, 9)], peer)

    g3[core * NZ + n, 0:9] = gp[core, 0:9]
    await_all(rcv.at[5], g3.at[pl.ds(0, 2 * NZ - 1), pl.ds(0, 9)])
    for part in (slice(0, 8), slice(8, 9)):
        total = g3[0, part]
        for i in range(1, 2 * NZ):
            total = total + g3[i, part]
        gsum[part] = total * (1.0 / float(RANK * RANK * RANK_FOUR))

    for peer in plane_peers():
        send(6, gsum.at[pl.ds(0, 9)], gfull.at[slot, pl.ds(0, 9)], peer)

    gfull[slot, 0:9] = gsum[0:9]
    await_all(rcv.at[2], b0g.at[pl.ds(0, NW - 1)])
    basis_t = b0g[...].reshape(256, 64).T
    await_all(rcv.at[6], gfull.at[pl.ds(0, NW - 1), pl.ds(0, 9)])

    for i in range(CHIPS):
        at = 16 * (i % 8)
        for c in range(2):
            body = gfull[2 * i + c, 0:8]
            if at:
                body = pltpu.roll(body, at, 1)
            last = jnp.broadcast_to(gfull[2 * i + c, 8:9], (8, 128))
            last = pltpu.roll(last, 0, 1, stride=16, stride_axis=0)
            if at:
                last = pltpu.roll(last, at, 1)
            near = jnp.where(lane >= at, body, 0.0)
            far = jnp.where(lane < at, body, jnp.where(lane < at + 16, last, 0.0))
            half = i // 8
            rows = slice(16 * i + 8 * c, 16 * i + 8 * c + 8)
            gmat[rows, 128 * half : 128 * half + 128] = near
            gmat[rows, 128 - 128 * half : 256 - 128 * half] = far
    half_gram = gmat[...]
    row_block = lax.broadcasted_iota(jnp.int32, (256, 256), 0) // 16
    column_block = lax.broadcasted_iota(jnp.int32, (256, 256), 1) // 16
    held = lax.rem(column_block - row_block + CHIPS, CHIPS) <= HALF
    gram = split3(jnp.where(held, half_gram, half_gram.T))
    for i in range(3):
        gparts[i] = gram[i]
    zt_ref[...] = mm_parts(split3(basis_t), gram, ((1,), (0,)))

    @pl.loop(0, ITERS)
    def _(step):
        zt = zt_ref[...]
        z = split3(zt)
        below = [jnp.concatenate([jnp.zeros((64, 256), v.dtype), v], axis=0) for v in z]
        linv = inverse_cholesky(mm_parts(z, below, ((1,), (1,))))
        linv_ref[...] = linv
        image_t = mm_parts(z, [gparts[i] for i in range(3)], ((1,), (0,)))

        @pl.when(step < ITERS - 1)
        def _():
            zt_ref[...] = mm_rows(linv, image_t, ((1,), (0,)))

    z_ref[...] = zt_ref[...].T
    mine = z_ref[pl.ds(pl.multiple_of(slot * 8, 8), 8), :]
    out_ref[...] = mm(mine, linv_ref[...], ((1,), (1,))) * math.sqrt(256.0)

    await_all(snd.at[0], f2g.at[pl.ds(0, CHIPS - 1)])
    await_all(snd.at[7], f2g.at[pl.ds(0, CHIPS)])
    await_all(snd.at[1], f3g.at[pl.ds(0, NZ - 1)])
    await_all(snd.at[2], b0g.at[pl.ds(0, NW - 1)])
    await_all(snd.at[3], r1.at[pl.ds(0, 2 * NZ - 1)])
    await_all(snd.at[4], a_ref.at[pl.ds(1, HALF)])
    await_all(snd.at[5], g3.at[pl.ds(0, 2 * NZ - 1), pl.ds(0, 9)])
    await_all(snd.at[6], gfull.at[pl.ds(0, NW - 1), pl.ds(0, 9)])


def per_device(tensor, factor_two, factor_three, factor_four, start_basis):
    f32, bf16 = jnp.float32, jnp.bfloat16
    x = tensor.reshape(8, 8, 128, 16, 4).transpose(0, 3, 1, 4, 2).reshape(4096, 128)
    hbm = pl.BlockSpec(memory_space=pltpu.HBM)
    operands = (x, factor_two, factor_three, factor_four.T, start_basis)
    return pl.pallas_call(
        kernel,
        out_shape=jax.ShapeDtypeStruct((8, 64), f32),
        in_specs=[hbm] * 5,
        out_specs=pl.BlockSpec(memory_space=pltpu.VMEM),
        scratch_shapes=[
            pltpu.VMEM((4096, 128), f32),
            pltpu.VMEM((32, 64), f32),
            pltpu.VMEM((16, 64), f32),
            pltpu.SMEM((2, 4), f32),
            pltpu.VMEM((8, 64), f32),
            pltpu.VMEM((16, 128), f32),
            pltpu.VMEM((NW, 16, 128), f32),
            pltpu.VMEM((NZ, 16, 64), f32),
            pltpu.VMEM((NW, 8, 64), f32),
            pltpu.VMEM((256, 1024), bf16),
            pltpu.VMEM((256, 1024), bf16),
            pltpu.VMEM((256, 1024), bf16),
            pltpu.VMEM((2, 8, 8, 128), f32),
            pltpu.VMEM((16, 8, 128), f32),
            pltpu.VMEM((128, 64), f32),
            pltpu.VMEM((16, 512), f32),
            pltpu.VMEM((HALF + 1, 16, 512), f32),
            pltpu.VMEM((2, 16, 128), f32),
            pltpu.VMEM((16, 16, 128), f32),
            pltpu.VMEM((16, 128), f32),
            pltpu.VMEM((NW, 16, 128), f32),
            pltpu.VMEM((256, 256), f32),
            pltpu.VMEM((3, 256, 256), bf16),
            pltpu.VMEM((64, 256), f32),
            pltpu.VMEM((256, 64), f32),
            pltpu.VMEM((64, 64), f32),
            pltpu.SemaphoreType.DMA((5,)),
            pltpu.SemaphoreType.DMA((8,)),
            pltpu.SemaphoreType.DMA((8,)),
        ],
        compiler_params=pltpu.CompilerParams(
            collective_id=0, has_side_effects=True, vmem_limit_bytes=40 * 2**20
        ),
        name="hooi",
    )(*(pltpu.with_memory_space_constraint(v, pltpu.HBM) for v in operands))


def solution(mesh):
    in_specs = (P("wa", None, "an", None), P("wa", None), P("an", None), P(), P("wa", None))
    return jax.shard_map(
        per_device, mesh=mesh, in_specs=in_specs, out_specs=P("wa", None), check_vma=False
    )
```

```python
import functools
import math

import jax
import jax.numpy as jnp
from jax import lax
from jax.experimental import pallas as pl
from jax.experimental.pallas import tpu as pltpu
from jax.sharding import PartitionSpec as P

RANK = 64
RANK_FOUR = 2
ITERS = 4
NW, NZ = 32, 8
CHIPS = NW // 2
HALF = CHIPS // 2
def hops(peer):
    x, y, z, c = peer
    return min(x, 4 - x) + min(y, 4 - y) + min(z, NZ - z) + 0.5 * c


EVERY = sorted(
    [
        (x, y, z, c)
        for x in range(4)
        for y in range(4)
        for z in range(NZ)
        for c in range(2)
        if (x or y or z or c) and not ((x or y) and z)
    ],
    key=hops,
    reverse=True,
)
PLANE = [(x, y, c) for x, y, z, c in EVERY if z == 0]
COLUMN = [(z, c) for x, y, z, c in EVERY if x == 0 and y == 0]


MESH = pl.DeviceIdType.MESH
HIGHEST = lax.Precision.HIGHEST


def split3(x):
    h = x.astype(jnp.bfloat16)
    rest = x - h.astype(jnp.float32)
    m = rest.astype(jnp.bfloat16)
    l = (rest - m.astype(jnp.float32)).astype(jnp.bfloat16)
    return h, m, l


def mm(a, b, dims=((1,), (0,))):
    return lax.dot_general(
        a, b, (dims, ((), ())), precision=HIGHEST, preferred_element_type=jnp.float32
    )


def mm16(a, b):
    return jnp.dot(a, b, preferred_element_type=jnp.float32)


def mm_parts(a, b, dims):
    def product(x, y):
        return lax.dot_general(x, y, (dims, ((), ())), preferred_element_type=jnp.float32)

    ah, am, al = a
    bh, bm, bl = b
    n = ah.shape[0]
    high = product(jnp.concatenate([ah, am, al], axis=0), bh)
    mid = product(jnp.concatenate([ah, am], axis=0), bm)
    low = product(ah, bl)
    return ((high[2 * n :] + low + mid[n:]) + (high[n : 2 * n] + mid[:n])) + high[:n]


def mm_rows(a, b, dims):
    return mm_parts(split3(a), split3(b), dims)


def lanes_of(tile, column):
    return jnp.broadcast_to(tile[:, column : column + 1], (8, 128))


def rows_of(tile, row):
    return jnp.broadcast_to(tile[row : row + 1, :], (8, 128))


def inverse_cholesky(wide):
    row = lax.broadcasted_iota(jnp.int32, (8, 128), 0)
    lane = lax.broadcasted_iota(jnp.int32, (8, 128), 1)
    s = [
        wide[8 * i : 8 * i + 8] + jnp.where(lane == row + 8 * i, 1.0, 0.0) for i in range(8)
    ]
    out = []
    ahead = [lanes_of(s[0], 64 + q) for q in range(8)]
    for t in range(8):
        cols = {
            i: [lanes_of(s[i], 64 + 8 * t + q) for q in range(8)] for i in range(t + 1, 8)
        }
        cols[t] = ahead
        if t < 7:
            ahead = [lanes_of(s[t + 1], 64 + 8 * (t + 1) + q) for q in range(8)]
        pivots = jnp.ones((8, 128), jnp.float32)
        for p in range(8):
            pivot_row = rows_of(s[t], p)
            pivot = rows_of(cols[t][p], p)
            inverse = 1.0 / pivot
            heads = [rows_of(cols[t][q], p) for q in range(8)]
            for i in range(t, 8):
                factor = cols[i][p] * inverse
                if i == t:
                    factor = jnp.where(row > p, factor, 0.0)
                if i == t + 1:
                    for q in range(8):
                        ahead[q] = ahead[q] - factor * rows_of(cols[i][p], q)
                s[i] = s[i] - factor * pivot_row
                for q in range(p + 1, 8):
                    cols[i][q] = cols[i][q] - factor * heads[q]
            pivots = jnp.where(row == p, pivot, pivots)
        out.append(s[t] * lax.rsqrt(pivots))
    return jnp.concatenate(out, axis=0)[:, 0:64]


def kernel(
    x_hbm, f2_hbm, f3_hbm, f4_hbm, b0_hbm, out_ref,
    xv, f2v, f3v, f4s, b0v, f2p, f2g, f3g, b0g, yh, ym, yl,
    s1, r1, vt, v_ref, a_ref, gp, g3, gsum, gfull, gmat, gparts, zt_ref, z_ref, linv_ref,
    loc, snd, rcv,
):
    w = lax.axis_index("wa")
    n = lax.axis_index("an")
    core = lax.rem(w, 2)
    chip = w // 2
    label = lax.rem(7 * chip, CHIPS)
    slot = label * 2 + core

    local = [
        pltpu.make_async_copy(f2_hbm, f2v, loc.at[0]),
        pltpu.make_async_copy(f3_hbm, f3v, loc.at[1]),
        pltpu.make_async_copy(b0_hbm, b0v, loc.at[2]),
        pltpu.make_async_copy(f4_hbm, f4s, loc.at[3]),
        pltpu.make_async_copy(x_hbm, xv, loc.at[4]),
    ]
    local[0].start()

    barrier = pltpu.get_barrier_semaphore()

    def plane_peers():
        for dx, dy, dc in PLANE:
            to = lax.rem(chip // 4 + dx, 4) * 4 + lax.rem(chip + dy, 4)
            yield to * 2 + lax.rem(core + dc, 2), n

    def column_peers():
        for dz, dc in COLUMN:
            to = lax.rem(core + dc, 2)
            yield to, (chip * 2 + to, lax.rem(n + dz, NZ))

    for dx, dy, dz, dc in EVERY:
        to = lax.rem(chip // 4 + dx, 4) * 4 + lax.rem(chip + dy, 4)
        peer = to * 2 + lax.rem(core + dc, 2), lax.rem(n + dz, NZ)
        pl.semaphore_signal(barrier, inc=1, device_id=peer, device_id_type=MESH)

    for copy in local[1:]:
        copy.start()
    local[0].wait()
    f2p[:, 0:64] = f2v[0:16, :]
    f2p[:, 64:128] = f2v[16:32, :]
    f2g[w] = f2p[...]

    pl.semaphore_wait(barrier, NW - 1 + 2 * NZ - 2)

    def send(stage, src, dst, peer):
        pltpu.make_async_remote_copy(
            src_ref=src, dst_ref=dst, send_sem=snd.at[stage], recv_sem=rcv.at[stage],
            device_id=peer, device_id_type=MESH,
        ).start()

    def await_all(sem, blocks):
        pltpu.make_async_copy(blocks, blocks, sem).wait()

    for peer in plane_peers():
        send(0, f2p, f2g.at[w], peer)

    local[1].wait()
    @pl.loop(1, NZ)
    def _(k):
        send(1, f3v, f3g.at[n], (w, lax.rem(n + k, NZ)))

    local[2].wait()
    f3g[n] = f3v[...]
    b0g[slot] = b0v[...]

    local[3].wait()
    local[4].wait()
    for bt in range(8):
        parts = [xv[pl.ds(bt * 4 + d, 128, stride=32), :] for d in range(4)]
        for g in range(2):
            total = parts[0] * f4s[g, 0]
            for d in range(1, 4):
                total = total + parts[d] * f4s[g, d]
            h, m, l = split3(total)
            here = (slice(128 * g, 128 * g + 128), slice(128 * bt, 128 * bt + 128))
            yh[here] = h
            ym[here] = m
            yl[here] = l

    await_all(rcv.at[0], f2g.at[pl.ds(0, NW - 1)])
    wh, wm, wl = (
        jnp.concatenate([v[:, :, 0:64], v[:, :, 64:128]], axis=1).reshape(1024, 64)
        for v in split3(f2g[...])
    )
    p0 = mm16(yh[...], jnp.concatenate([wh, wm, wl], axis=1))
    p1 = mm16(ym[...], jnp.concatenate([wh, wm], axis=1))
    p2 = mm16(yl[...], wh)
    first = (p0[:, 128:192] + p1[:, 64:128] + p2) + (p0[:, 64:128] + p1[:, 0:64]) + p0[:, 0:64]
    for g in range(2):
        s1[g] = first[128 * g : 128 * g + 128].T.reshape(8, 8, 128)

    for to, peer in column_peers():
        send(3, s1.at[to, peer[1]], r1.at[core * NZ + n], peer)

    for peer in plane_peers():
        send(2, b0v, b0g.at[slot], peer)

    r1[core * NZ + n] = s1[core, n]
    await_all(rcv.at[1], f3g.at[pl.ds(0, NZ - 1)])
    full_three = f3g[...].reshape(128, 64)
    await_all(rcv.at[3], r1.at[pl.ds(0, 2 * NZ - 1)])

    lane = lax.broadcasted_iota(jnp.int32, (8, 128), 1)
    rows = []
    for s in range(2):
        v = [r1[s * NZ + m] for m in range(NZ)]
        for d in (4, 2, 1):
            upper = lax.rem(lane // (16 * d), 2) == 1
            nxt = list(v)
            for i in range(8):
                if i & d == 0:
                    j = i + d
                    nxt[i] = jnp.where(upper, pltpu.roll(v[j], 16 * d, 1), v[i])
                    nxt[j] = jnp.where(upper, v[j], pltpu.roll(v[i], 128 - 16 * d, 1))
            v = nxt
        rows += v
    vt[...] = mm(jnp.concatenate(rows, axis=0), full_three)
    for e in range(8):
        v_ref[:, 64 * e : 64 * e + 64] = vt[pl.ds(e, 16, stride=8), :]

    for k in (1, 3, 6, 2, 5, 7, 8, 4):
        to = lax.rem(7 * lax.rem(label + CHIPS - k, CHIPS), CHIPS)
        send(4, v_ref, a_ref.at[k], (to * 2 + core, n))

    a_ref[0] = v_ref[...]
    await_all(rcv.at[4], a_ref.at[pl.ds(1, HALF)])
    partial = mm_rows(v_ref[...], a_ref[...].reshape(144, 512), ((1,), (1,)))
    row = lax.broadcasted_iota(jnp.int32, (8, 128), 0)
    for s in range(2):
        gp[s, 0:8] = partial[8 * s : 8 * s + 8, 0:128]
        last = jnp.concatenate([partial[8 * s : 8 * s + 8, 128:144]] * 8, axis=1)
        gp[s, 8:9] = jnp.sum(jnp.where(lane // 16 == lax.rem(8 - row, 8), last, 0.0), axis=0, keepdims=True)

    for to, peer in column_peers():
        send(5, gp.at[to, pl.ds(0, 9)], g3.at[core * NZ + n, pl.ds(0, 9)], peer)

    g3[core * NZ + n, 0:9] = gp[core, 0:9]
    await_all(rcv.at[5], g3.at[pl.ds(0, 2 * NZ - 1), pl.ds(0, 9)])
    for part in (slice(0, 8), slice(8, 9)):
        total = g3[0, part]
        for i in range(1, 2 * NZ):
            total = total + g3[i, part]
        gsum[part] = total * (1.0 / float(RANK * RANK * RANK_FOUR))

    for peer in plane_peers():
        send(6, gsum.at[pl.ds(0, 9)], gfull.at[slot, pl.ds(0, 9)], peer)

    gfull[slot, 0:9] = gsum[0:9]
    await_all(rcv.at[2], b0g.at[pl.ds(0, NW - 1)])
    basis_t = b0g[...].reshape(256, 64).T
    await_all(rcv.at[6], gfull.at[pl.ds(0, NW - 1), pl.ds(0, 9)])

    for i in range(CHIPS):
        at = 16 * (i % 8)
        for c in range(2):
            body = gfull[2 * i + c, 0:8]
            if at:
                body = pltpu.roll(body, at, 1)
            last = jnp.broadcast_to(gfull[2 * i + c, 8:9], (8, 128))
            last = pltpu.roll(last, 0, 1, stride=16, stride_axis=0)
            if at:
                last = pltpu.roll(last, at, 1)
            near = jnp.where(lane >= at, body, 0.0)
            far = jnp.where(lane < at, body, jnp.where(lane < at + 16, last, 0.0))
            half = i // 8
            rows = slice(16 * i + 8 * c, 16 * i + 8 * c + 8)
            gmat[rows, 128 * half : 128 * half + 128] = near
            gmat[rows, 128 - 128 * half : 256 - 128 * half] = far
    half_gram = gmat[...]
    row_block = lax.broadcasted_iota(jnp.int32, (256, 256), 0) // 16
    column_block = lax.broadcasted_iota(jnp.int32, (256, 256), 1) // 16
    held = lax.rem(column_block - row_block + CHIPS, CHIPS) <= HALF
    gram = split3(jnp.where(held, half_gram, half_gram.T))
    for i in range(3):
        gparts[i] = gram[i]
    zt_ref[...] = mm_parts(split3(basis_t), gram, ((1,), (0,)))

    @pl.loop(0, ITERS)
    def _(step):
        zt = zt_ref[...]
        z = split3(zt)
        below = [jnp.concatenate([jnp.zeros((64, 256), v.dtype), v], axis=0) for v in z]
        linv = inverse_cholesky(mm_parts(z, below, ((1,), (1,))))
        linv_ref[...] = linv
        image_t = mm_parts(z, [gparts[i] for i in range(3)], ((1,), (0,)))

        @pl.when(step < ITERS - 1)
        def _():
            zt_ref[...] = mm_rows(linv, image_t, ((1,), (0,)))

    z_ref[...] = zt_ref[...].T
    mine = z_ref[pl.ds(pl.multiple_of(slot * 8, 8), 8), :]
    out_ref[...] = mm(mine, linv_ref[...], ((1,), (1,))) * math.sqrt(256.0)

    await_all(snd.at[0], f2g.at[pl.ds(0, NW - 1)])
    await_all(snd.at[1], f3g.at[pl.ds(0, NZ - 1)])
    await_all(snd.at[2], b0g.at[pl.ds(0, NW - 1)])
    await_all(snd.at[3], r1.at[pl.ds(0, 2 * NZ - 1)])
    await_all(snd.at[4], a_ref.at[pl.ds(1, HALF)])
    await_all(snd.at[5], g3.at[pl.ds(0, 2 * NZ - 1), pl.ds(0, 9)])
    await_all(snd.at[6], gfull.at[pl.ds(0, NW - 1), pl.ds(0, 9)])


def per_device(tensor, factor_two, factor_three, factor_four, start_basis):
    f32, bf16 = jnp.float32, jnp.bfloat16
    x = tensor.reshape(8, 8, 128, 16, 4).transpose(0, 3, 1, 4, 2).reshape(4096, 128)
    hbm = pl.BlockSpec(memory_space=pltpu.HBM)
    operands = (x, factor_two, factor_three, factor_four.T, start_basis)
    return pl.pallas_call(
        kernel,
        out_shape=jax.ShapeDtypeStruct((8, 64), f32),
        in_specs=[hbm] * 5,
        out_specs=pl.BlockSpec(memory_space=pltpu.VMEM),
        scratch_shapes=[
            pltpu.VMEM((4096, 128), f32),
            pltpu.VMEM((32, 64), f32),
            pltpu.VMEM((16, 64), f32),
            pltpu.SMEM((2, 4), f32),
            pltpu.VMEM((8, 64), f32),
            pltpu.VMEM((16, 128), f32),
            pltpu.VMEM((NW, 16, 128), f32),
            pltpu.VMEM((NZ, 16, 64), f32),
            pltpu.VMEM((NW, 8, 64), f32),
            pltpu.VMEM((256, 1024), bf16),
            pltpu.VMEM((256, 1024), bf16),
            pltpu.VMEM((256, 1024), bf16),
            pltpu.VMEM((2, 8, 8, 128), f32),
            pltpu.VMEM((16, 8, 128), f32),
            pltpu.VMEM((128, 64), f32),
            pltpu.VMEM((16, 512), f32),
            pltpu.VMEM((HALF + 1, 16, 512), f32),
            pltpu.VMEM((2, 16, 128), f32),
            pltpu.VMEM((16, 16, 128), f32),
            pltpu.VMEM((16, 128), f32),
            pltpu.VMEM((NW, 16, 128), f32),
            pltpu.VMEM((256, 256), f32),
            pltpu.VMEM((3, 256, 256), bf16),
            pltpu.VMEM((64, 256), f32),
            pltpu.VMEM((256, 64), f32),
            pltpu.VMEM((64, 64), f32),
            pltpu.SemaphoreType.DMA((5,)),
            pltpu.SemaphoreType.DMA((7,)),
            pltpu.SemaphoreType.DMA((7,)),
        ],
        compiler_params=pltpu.CompilerParams(
            collective_id=0, has_side_effects=True, vmem_limit_bytes=40 * 2**20
        ),
        name="hooi",
    )(*(pltpu.with_memory_space_constraint(v, pltpu.HBM) for v in operands))


def solution(mesh):
    in_specs = (P("wa", None, "an", None), P("wa", None), P("an", None), P(), P("wa", None))
    return jax.shard_map(
        per_device, mesh=mesh, in_specs=in_specs, out_specs=P("wa", None), check_vma=False
    )
```

```python
import functools
import math

import jax
import jax.numpy as jnp
from jax import lax
from jax.experimental import pallas as pl
from jax.experimental.pallas import tpu as pltpu
from jax.sharding import PartitionSpec as P

RANK = 64
RANK_FOUR = 2
ITERS = 4
NW, NZ = 32, 8
CHIPS = NW // 2
HALF = CHIPS // 2
def hops(peer):
    x, y, z, c = peer
    return min(x, 4 - x) + min(y, 4 - y) + min(z, NZ - z) + 0.5 * c


EVERY = sorted(
    [
        (x, y, z, c)
        for x in range(4)
        for y in range(4)
        for z in range(NZ)
        for c in range(2)
        if (x or y or z or c) and not ((x or y) and z)
    ],
    key=hops,
    reverse=True,
)
PLANE = [(x, y, c) for x, y, z, c in EVERY if z == 0]
COLUMN = [(z, c) for x, y, z, c in EVERY if x == 0 and y == 0]


MESH = pl.DeviceIdType.MESH
HIGHEST = lax.Precision.HIGHEST


def split3(x):
    h = x.astype(jnp.bfloat16)
    rest = x - h.astype(jnp.float32)
    m = rest.astype(jnp.bfloat16)
    l = (rest - m.astype(jnp.float32)).astype(jnp.bfloat16)
    return h, m, l


def mm(a, b, dims=((1,), (0,))):
    return lax.dot_general(
        a, b, (dims, ((), ())), precision=HIGHEST, preferred_element_type=jnp.float32
    )


def mm16(a, b):
    return jnp.dot(a, b, preferred_element_type=jnp.float32)


def mm_parts(a, b, dims):
    def product(x, y):
        return lax.dot_general(x, y, (dims, ((), ())), preferred_element_type=jnp.float32)

    ah, am, al = a
    bh, bm, bl = b
    n = ah.shape[0]
    high = product(jnp.concatenate([ah, am, al], axis=0), bh)
    mid = product(jnp.concatenate([ah, am], axis=0), bm)
    low = product(ah, bl)
    return ((high[2 * n :] + low + mid[n:]) + (high[n : 2 * n] + mid[:n])) + high[:n]


def mm_rows(a, b, dims):
    return mm_parts(split3(a), split3(b), dims)


def lanes_of(tile, column):
    return jnp.broadcast_to(tile[:, column : column + 1], (8, 128))


def rows_of(tile, row):
    return jnp.broadcast_to(tile[row : row + 1, :], (8, 128))


def inverse_cholesky(wide):
    row = lax.broadcasted_iota(jnp.int32, (8, 128), 0)
    lane = lax.broadcasted_iota(jnp.int32, (8, 128), 1)
    s = [
        wide[8 * i : 8 * i + 8] + jnp.where(lane == row + 8 * i, 1.0, 0.0) for i in range(8)
    ]
    out = []
    ahead = [lanes_of(s[0], 64 + q) for q in range(8)]
    for t in range(8):
        cols = {
            i: [lanes_of(s[i], 64 + 8 * t + q) for q in range(8)] for i in range(t + 1, 8)
        }
        cols[t] = ahead
        if t < 7:
            ahead = [lanes_of(s[t + 1], 64 + 8 * (t + 1) + q) for q in range(8)]
        pivots = jnp.ones((8, 128), jnp.float32)
        later = {i: [] for i in range(t + 2, 8)}
        for p in range(8):
            pivot_row = rows_of(s[t], p)
            pivot = rows_of(cols[t][p], p)
            inverse = 1.0 / pivot
            heads = [rows_of(cols[t][q], p) for q in range(8)]
            for i in range(t, 8):
                factor = cols[i][p] * inverse
                if i == t:
                    factor = jnp.where(row > p, factor, 0.0)
                if i == t + 1:
                    for q in range(8):
                        ahead[q] = ahead[q] - factor * rows_of(cols[i][p], q)
                if i < t + 2:
                    s[i] = s[i] - factor * pivot_row
                else:
                    later[i].append(factor * pivot_row)
                for q in range(p + 1, 8):
                    cols[i][q] = cols[i][q] - factor * heads[q]
            pivots = jnp.where(row == p, pivot, pivots)
        for i, v in later.items():
            s[i] = s[i] - (((v[0] + v[1]) + (v[2] + v[3])) + ((v[4] + v[5]) + (v[6] + v[7])))
        out.append(s[t] * lax.rsqrt(pivots))
    return jnp.concatenate(out, axis=0)[:, 0:64]


def kernel(
    x_hbm, f2_hbm, f3_hbm, f4_hbm, b0_hbm, out_ref,
    xv, f2v, f3v, f4s, b0v, f2p, f2g, f3g, b0g, yh, ym, yl,
    s1, r1, vt, v_ref, a_ref, gp, g3, gsum, gfull, gmat, gparts, zt_ref, z_ref, linv_ref,
    loc, snd, rcv,
):
    w = lax.axis_index("wa")
    n = lax.axis_index("an")
    core = lax.rem(w, 2)
    chip = w // 2
    label = lax.rem(7 * chip, CHIPS)
    slot = label * 2 + core

    local = [
        pltpu.make_async_copy(f2_hbm, f2v, loc.at[0]),
        pltpu.make_async_copy(f3_hbm, f3v, loc.at[1]),
        pltpu.make_async_copy(b0_hbm, b0v, loc.at[2]),
        pltpu.make_async_copy(f4_hbm, f4s, loc.at[3]),
        pltpu.make_async_copy(x_hbm, xv, loc.at[4]),
    ]
    local[0].start()

    barrier = pltpu.get_barrier_semaphore()

    def plane_peers():
        for dx, dy, dc in PLANE:
            to = lax.rem(chip // 4 + dx, 4) * 4 + lax.rem(chip + dy, 4)
            yield to * 2 + lax.rem(core + dc, 2), n

    def column_peers():
        for dz, dc in COLUMN:
            to = lax.rem(core + dc, 2)
            yield to, (chip * 2 + to, lax.rem(n + dz, NZ))

    for dx, dy, dz, dc in EVERY:
        to = lax.rem(chip // 4 + dx, 4) * 4 + lax.rem(chip + dy, 4)
        peer = to * 2 + lax.rem(core + dc, 2), lax.rem(n + dz, NZ)
        pl.semaphore_signal(barrier, inc=1, device_id=peer, device_id_type=MESH)

    for copy in local[1:]:
        copy.start()
    local[0].wait()
    f2p[:, 0:64] = f2v[0:16, :]
    f2p[:, 64:128] = f2v[16:32, :]
    f2g[w] = f2p[...]

    pl.semaphore_wait(barrier, NW - 1 + 2 * NZ - 2)

    def send(stage, src, dst, peer):
        pltpu.make_async_remote_copy(
            src_ref=src, dst_ref=dst, send_sem=snd.at[stage], recv_sem=rcv.at[stage],
            device_id=peer, device_id_type=MESH,
        ).start()

    def await_all(sem, blocks):
        pltpu.make_async_copy(blocks, blocks, sem).wait()

    for peer in plane_peers():
        send(0, f2p, f2g.at[w], peer)

    local[1].wait()
    @pl.loop(1, NZ)
    def _(k):
        send(1, f3v, f3g.at[n], (w, lax.rem(n + k, NZ)))

    local[2].wait()
    f3g[n] = f3v[...]
    b0g[slot] = b0v[...]

    local[3].wait()
    local[4].wait()
    for bt in range(8):
        parts = [xv[pl.ds(bt * 4 + d, 128, stride=32), :] for d in range(4)]
        for g in range(2):
            total = parts[0] * f4s[g, 0]
            for d in range(1, 4):
                total = total + parts[d] * f4s[g, d]
            h, m, l = split3(total)
            here = (slice(128 * g, 128 * g + 128), slice(128 * bt, 128 * bt + 128))
            yh[here] = h
            ym[here] = m
            yl[here] = l

    await_all(rcv.at[0], f2g.at[pl.ds(0, NW - 1)])
    wh, wm, wl = (
        jnp.concatenate([v[:, :, 0:64], v[:, :, 64:128]], axis=1).reshape(1024, 64)
        for v in split3(f2g[...])
    )
    p0 = mm16(yh[...], jnp.concatenate([wh, wm, wl], axis=1))
    p1 = mm16(ym[...], jnp.concatenate([wh, wm], axis=1))
    p2 = mm16(yl[...], wh)
    first = (p0[:, 128:192] + p1[:, 64:128] + p2) + (p0[:, 64:128] + p1[:, 0:64]) + p0[:, 0:64]
    for g in range(2):
        s1[g] = first[128 * g : 128 * g + 128].T.reshape(8, 8, 128)

    for to, peer in column_peers():
        send(3, s1.at[to, peer[1]], r1.at[core * NZ + n], peer)

    r1[core * NZ + n] = s1[core, n]
    await_all(rcv.at[1], f3g.at[pl.ds(0, NZ - 1)])
    full_three = f3g[...].reshape(128, 64)
    await_all(rcv.at[3], r1.at[pl.ds(0, 2 * NZ - 1)])

    lane = lax.broadcasted_iota(jnp.int32, (8, 128), 1)
    rows = []
    for s in range(2):
        v = [r1[s * NZ + m] for m in range(NZ)]
        for d in (4, 2, 1):
            upper = lax.rem(lane // (16 * d), 2) == 1
            nxt = list(v)
            for i in range(8):
                if i & d == 0:
                    j = i + d
                    nxt[i] = jnp.where(upper, pltpu.roll(v[j], 16 * d, 1), v[i])
                    nxt[j] = jnp.where(upper, v[j], pltpu.roll(v[i], 128 - 16 * d, 1))
            v = nxt
        rows += v
    vt[...] = mm(jnp.concatenate(rows, axis=0), full_three)
    for e in range(8):
        v_ref[:, 64 * e : 64 * e + 64] = vt[pl.ds(e, 16, stride=8), :]

    for k in (1, 3, 6, 2, 5, 7, 8, 4):
        to = lax.rem(7 * lax.rem(label + CHIPS - k, CHIPS), CHIPS)
        send(4, v_ref, a_ref.at[k], (to * 2 + core, n))

    a_ref[0] = v_ref[...]
    await_all(rcv.at[4], a_ref.at[pl.ds(1, HALF)])
    partial = mm_rows(v_ref[...], a_ref[...].reshape(144, 512), ((1,), (1,)))
    row = lax.broadcasted_iota(jnp.int32, (8, 128), 0)
    for s in range(2):
        gp[s, 0:8] = partial[8 * s : 8 * s + 8, 0:128]
        last = jnp.concatenate([partial[8 * s : 8 * s + 8, 128:144]] * 8, axis=1)
        gp[s, 8:9] = jnp.sum(jnp.where(lane // 16 == lax.rem(8 - row, 8), last, 0.0), axis=0, keepdims=True)

    for to, peer in column_peers():
        send(5, gp.at[to, pl.ds(0, 9)], g3.at[core * NZ + n, pl.ds(0, 9)], peer)

    for peer in plane_peers():
        send(2, b0v, b0g.at[slot], peer)

    g3[core * NZ + n, 0:9] = gp[core, 0:9]
    await_all(rcv.at[5], g3.at[pl.ds(0, 2 * NZ - 1), pl.ds(0, 9)])
    for part in (slice(0, 8), slice(8, 9)):
        total = g3[0, part]
        for i in range(1, 2 * NZ):
            total = total + g3[i, part]
        gsum[part] = total * (1.0 / float(RANK * RANK * RANK_FOUR))

    for peer in plane_peers():
        send(6, gsum.at[pl.ds(0, 9)], gfull.at[slot, pl.ds(0, 9)], peer)

    gfull[slot, 0:9] = gsum[0:9]
    await_all(rcv.at[2], b0g.at[pl.ds(0, NW - 1)])
    basis_t = b0g[...].reshape(256, 64).T
    await_all(rcv.at[6], gfull.at[pl.ds(0, NW - 1), pl.ds(0, 9)])

    for i in range(CHIPS):
        at = 16 * (i % 8)
        for c in range(2):
            body = gfull[2 * i + c, 0:8]
            if at:
                body = pltpu.roll(body, at, 1)
            last = jnp.broadcast_to(gfull[2 * i + c, 8:9], (8, 128))
            last = pltpu.roll(last, 0, 1, stride=16, stride_axis=0)
            if at:
                last = pltpu.roll(last, at, 1)
            near = jnp.where(lane >= at, body, 0.0)
            far = jnp.where(lane < at, body, jnp.where(lane < at + 16, last, 0.0))
            half = i // 8
            rows = slice(16 * i + 8 * c, 16 * i + 8 * c + 8)
            gmat[rows, 128 * half : 128 * half + 128] = near
            gmat[rows, 128 - 128 * half : 256 - 128 * half] = far
    half_gram = gmat[...]
    row_block = lax.broadcasted_iota(jnp.int32, (256, 256), 0) // 16
    column_block = lax.broadcasted_iota(jnp.int32, (256, 256), 1) // 16
    held = lax.rem(column_block - row_block + CHIPS, CHIPS) <= HALF
    gram = split3(jnp.where(held, half_gram, half_gram.T))
    for i in range(3):
        gparts[i] = gram[i]
    zt_ref[...] = mm_parts(split3(basis_t), gram, ((1,), (0,)))

    @pl.loop(0, ITERS)
    def _(step):
        zt = zt_ref[...]
        z = split3(zt)
        below = [jnp.concatenate([jnp.zeros((64, 256), v.dtype), v], axis=0) for v in z]
        linv = inverse_cholesky(mm_parts(z, below, ((1,), (1,))))
        linv_ref[...] = linv
        image_t = mm_parts(z, [gparts[i] for i in range(3)], ((1,), (0,)))

        @pl.when(step < ITERS - 1)
        def _():
            zt_ref[...] = mm_rows(linv, image_t, ((1,), (0,)))

    z_ref[...] = zt_ref[...].T
    mine = z_ref[pl.ds(pl.multiple_of(slot * 8, 8), 8), :]
    out_ref[...] = mm(mine, linv_ref[...], ((1,), (1,))) * math.sqrt(256.0)

    await_all(snd.at[0], f2g.at[pl.ds(0, NW - 1)])
    await_all(snd.at[1], f3g.at[pl.ds(0, NZ - 1)])
    await_all(snd.at[2], b0g.at[pl.ds(0, NW - 1)])
    await_all(snd.at[3], r1.at[pl.ds(0, 2 * NZ - 1)])
    await_all(snd.at[4], a_ref.at[pl.ds(1, HALF)])
    await_all(snd.at[5], g3.at[pl.ds(0, 2 * NZ - 1), pl.ds(0, 9)])
    await_all(snd.at[6], gfull.at[pl.ds(0, NW - 1), pl.ds(0, 9)])


def per_device(tensor, factor_two, factor_three, factor_four, start_basis):
    f32, bf16 = jnp.float32, jnp.bfloat16
    x = tensor.reshape(8, 8, 128, 16, 4).transpose(0, 3, 1, 4, 2).reshape(4096, 128)
    hbm = pl.BlockSpec(memory_space=pltpu.HBM)
    operands = (x, factor_two, factor_three, factor_four.T, start_basis)
    return pl.pallas_call(
        kernel,
        out_shape=jax.ShapeDtypeStruct((8, 64), f32),
        in_specs=[hbm] * 5,
        out_specs=pl.BlockSpec(memory_space=pltpu.VMEM),
        scratch_shapes=[
            pltpu.VMEM((4096, 128), f32),
            pltpu.VMEM((32, 64), f32),
            pltpu.VMEM((16, 64), f32),
            pltpu.SMEM((2, 4), f32),
            pltpu.VMEM((8, 64), f32),
            pltpu.VMEM((16, 128), f32),
            pltpu.VMEM((NW, 16, 128), f32),
            pltpu.VMEM((NZ, 16, 64), f32),
            pltpu.VMEM((NW, 8, 64), f32),
            pltpu.VMEM((256, 1024), bf16),
            pltpu.VMEM((256, 1024), bf16),
            pltpu.VMEM((256, 1024), bf16),
            pltpu.VMEM((2, 8, 8, 128), f32),
            pltpu.VMEM((16, 8, 128), f32),
            pltpu.VMEM((128, 64), f32),
            pltpu.VMEM((16, 512), f32),
            pltpu.VMEM((HALF + 1, 16, 512), f32),
            pltpu.VMEM((2, 16, 128), f32),
            pltpu.VMEM((16, 16, 128), f32),
            pltpu.VMEM((16, 128), f32),
            pltpu.VMEM((NW, 16, 128), f32),
            pltpu.VMEM((256, 256), f32),
            pltpu.VMEM((3, 256, 256), bf16),
            pltpu.VMEM((64, 256), f32),
            pltpu.VMEM((256, 64), f32),
            pltpu.VMEM((64, 64), f32),
            pltpu.SemaphoreType.DMA((5,)),
            pltpu.SemaphoreType.DMA((7,)),
            pltpu.SemaphoreType.DMA((7,)),
        ],
        compiler_params=pltpu.CompilerParams(
            collective_id=0, has_side_effects=True, vmem_limit_bytes=40 * 2**20
        ),
        name="hooi",
    )(*(pltpu.with_memory_space_constraint(v, pltpu.HBM) for v in operands))


def solution(mesh):
    in_specs = (P("wa", None, "an", None), P("wa", None), P("an", None), P(), P("wa", None))
    return jax.shard_map(
        per_device, mesh=mesh, in_specs=in_specs, out_specs=P("wa", None), check_vma=False
    )
```

```python
import functools
import math

import jax
import jax.numpy as jnp
from jax import lax
from jax.experimental import pallas as pl
from jax.experimental.pallas import tpu as pltpu
from jax.sharding import PartitionSpec as P

RANK = 64
RANK_FOUR = 2
ITERS = 4
NW, NZ = 32, 8
CHIPS = NW // 2
HALF = CHIPS // 2
def hops(peer):
    x, y, z, c = peer
    return min(x, 4 - x) + min(y, 4 - y) + min(z, NZ - z) + 0.5 * c


EVERY = sorted(
    [
        (x, y, z, c)
        for x in range(4)
        for y in range(4)
        for z in range(NZ)
        for c in range(2)
        if (x or y or z or c) and not ((x or y) and z)
    ],
    key=hops,
    reverse=True,
)
PLANE = [(x, y, c) for x, y, z, c in EVERY if z == 0]
COLUMN = [(z, c) for x, y, z, c in EVERY if x == 0 and y == 0]


MESH = pl.DeviceIdType.MESH
HIGHEST = lax.Precision.HIGHEST


def split3(x):
    h = x.astype(jnp.bfloat16)
    rest = x - h.astype(jnp.float32)
    m = rest.astype(jnp.bfloat16)
    l = (rest - m.astype(jnp.float32)).astype(jnp.bfloat16)
    return h, m, l


def mm(a, b, dims=((1,), (0,))):
    return lax.dot_general(
        a, b, (dims, ((), ())), precision=HIGHEST, preferred_element_type=jnp.float32
    )


def mm16(a, b):
    return jnp.dot(a, b, preferred_element_type=jnp.float32)


def mm_parts(a, b, dims):
    def product(x, y):
        return lax.dot_general(x, y, (dims, ((), ())), preferred_element_type=jnp.float32)

    ah, am, al = a
    bh, bm, bl = b
    n = ah.shape[0]
    high = product(jnp.concatenate([ah, am, al], axis=0), bh)
    mid = product(jnp.concatenate([ah, am], axis=0), bm)
    low = product(ah, bl)
    return ((high[2 * n :] + low + mid[n:]) + (high[n : 2 * n] + mid[:n])) + high[:n]


def mm_rows(a, b, dims):
    return mm_parts(split3(a), split3(b), dims)


def lanes_of(tile, column):
    return jnp.broadcast_to(tile[:, column : column + 1], (8, 128))


def rows_of(tile, row):
    return jnp.broadcast_to(tile[row : row + 1, :], (8, 128))


def inverse_cholesky(wide):
    row = lax.broadcasted_iota(jnp.int32, (8, 128), 0)
    lane = lax.broadcasted_iota(jnp.int32, (8, 128), 1)
    s = [
        wide[8 * i : 8 * i + 8] + jnp.where(lane == row + 8 * i, 1.0, 0.0) for i in range(8)
    ]
    out = []
    ahead = [lanes_of(s[0], 64 + q) for q in range(8)]
    for t in range(8):
        cols = {
            i: [lanes_of(s[i], 64 + 8 * t + q) for q in range(8)] for i in range(t + 1, 8)
        }
        cols[t] = ahead
        if t < 7:
            ahead = [lanes_of(s[t + 1], 64 + 8 * (t + 1) + q) for q in range(8)]
        pivots = jnp.ones((8, 128), jnp.float32)
        later = {i: [] for i in range(t + 2, 8)}
        for p in range(8):
            pivot_row = rows_of(s[t], p)
            pivot = rows_of(cols[t][p], p)
            inverse = 1.0 / pivot
            heads = [rows_of(cols[t][q], p) for q in range(8)]
            for i in range(t, 8):
                factor = cols[i][p] * inverse
                if i == t:
                    factor = jnp.where(row > p, factor, 0.0)
                if i == t + 1:
                    for q in range(8):
                        ahead[q] = ahead[q] - factor * rows_of(cols[i][p], q)
                if i < t + 2:
                    s[i] = s[i] - factor * pivot_row
                else:
                    later[i].append(factor * pivot_row)
                for q in range(p + 1, 8):
                    cols[i][q] = cols[i][q] - factor * heads[q]
            pivots = jnp.where(row == p, pivot, pivots)
        for i, v in later.items():
            s[i] = s[i] - (((v[0] + v[1]) + (v[2] + v[3])) + ((v[4] + v[5]) + (v[6] + v[7])))
        out.append(s[t] * lax.rsqrt(pivots))
    return jnp.concatenate(out, axis=0)[:, 0:64]


def kernel(
    x_hbm, f2_hbm, f3_hbm, f4_hbm, b0_hbm, out_ref,
    xv, f2v, f3v, f4s, b0v, f2p, f2g, f3g, b0g, yh, ym, yl,
    s1, r1, vt, v_ref, a_ref, gp, g3, gsum, gfull, gmat, gparts, zt_ref, z_ref, linv_ref,
    loc, snd, rcv,
):
    w = lax.axis_index("wa")
    n = lax.axis_index("an")
    core = lax.rem(w, 2)
    chip = w // 2
    label = lax.rem(7 * chip, CHIPS)
    slot = label * 2 + core

    local = [
        pltpu.make_async_copy(f2_hbm, f2v, loc.at[0]),
        pltpu.make_async_copy(f3_hbm, f3v, loc.at[1]),
        pltpu.make_async_copy(b0_hbm, b0v, loc.at[2]),
        pltpu.make_async_copy(f4_hbm, f4s, loc.at[3]),
        pltpu.make_async_copy(x_hbm, xv, loc.at[4]),
    ]
    local[0].start()

    barrier = pltpu.get_barrier_semaphore()

    def plane_peers():
        for dx, dy, dc in PLANE:
            to = lax.rem(chip // 4 + dx, 4) * 4 + lax.rem(chip + dy, 4)
            yield to * 2 + lax.rem(core + dc, 2), n

    def column_peers():
        for dz, dc in COLUMN:
            to = lax.rem(core + dc, 2)
            yield to, (chip * 2 + to, lax.rem(n + dz, NZ))

    for dx, dy, dz, dc in EVERY:
        to = lax.rem(chip // 4 + dx, 4) * 4 + lax.rem(chip + dy, 4)
        peer = to * 2 + lax.rem(core + dc, 2), lax.rem(n + dz, NZ)
        pl.semaphore_signal(barrier, inc=1, device_id=peer, device_id_type=MESH)

    for copy in local[1:]:
        copy.start()
    local[0].wait()
    f2p[:, 0:64] = f2v[0:16, :]
    f2p[:, 64:128] = f2v[16:32, :]
    f2g[w] = f2p[...]

    pl.semaphore_wait(barrier, NW - 1 + 2 * NZ - 2)

    def send(stage, src, dst, peer):
        pltpu.make_async_remote_copy(
            src_ref=src, dst_ref=dst, send_sem=snd.at[stage], recv_sem=rcv.at[stage],
            device_id=peer, device_id_type=MESH,
        ).start()

    def await_all(sem, blocks):
        pltpu.make_async_copy(blocks, blocks, sem).wait()

    for peer in plane_peers():
        send(0, f2p, f2g.at[w], peer)

    local[1].wait()
    @pl.loop(1, NZ)
    def _(k):
        send(1, f3v, f3g.at[n], (w, lax.rem(n + k, NZ)))

    local[2].wait()
    f3g[n] = f3v[...]
    b0g[slot] = b0v[...]

    local[3].wait()
    local[4].wait()
    for bt in range(8):
        parts = [xv[pl.ds(bt * 4 + d, 128, stride=32), :] for d in range(4)]
        for g in range(2):
            total = parts[0] * f4s[g, 0]
            for d in range(1, 4):
                total = total + parts[d] * f4s[g, d]
            h, m, l = split3(total)
            here = (slice(128 * g, 128 * g + 128), slice(128 * bt, 128 * bt + 128))
            yh[here] = h
            ym[here] = m
            yl[here] = l

    await_all(rcv.at[0], f2g.at[pl.ds(0, NW - 1)])
    wh, wm, wl = (
        jnp.concatenate([v[:, :, 0:64], v[:, :, 64:128]], axis=1).reshape(1024, 64)
        for v in split3(f2g[...])
    )
    p0 = mm16(yh[...], jnp.concatenate([wh, wm, wl], axis=1))
    p1 = mm16(ym[...], jnp.concatenate([wh, wm], axis=1))
    p2 = mm16(yl[...], wh)
    first = (p0[:, 128:192] + p1[:, 64:128] + p2) + (p0[:, 64:128] + p1[:, 0:64]) + p0[:, 0:64]
    for g in range(2):
        s1[g] = first[128 * g : 128 * g + 128].T.reshape(8, 8, 128)

    for to, peer in column_peers():
        send(3, s1.at[to, peer[1]], r1.at[core * NZ + n], peer)

    for peer in plane_peers():
        send(2, b0v, b0g.at[slot], peer)

    r1[core * NZ + n] = s1[core, n]
    await_all(rcv.at[1], f3g.at[pl.ds(0, NZ - 1)])
    full_three = f3g[...].reshape(128, 64)
    await_all(rcv.at[3], r1.at[pl.ds(0, 2 * NZ - 1)])

    lane = lax.broadcasted_iota(jnp.int32, (8, 128), 1)
    rows = []
    for s in range(2):
        v = [r1[s * NZ + m] for m in range(NZ)]
        for d in (4, 2, 1):
            upper = lax.rem(lane // (16 * d), 2) == 1
            nxt = list(v)
            for i in range(8):
                if i & d == 0:
                    j = i + d
                    nxt[i] = jnp.where(upper, pltpu.roll(v[j], 16 * d, 1), v[i])
                    nxt[j] = jnp.where(upper, v[j], pltpu.roll(v[i], 128 - 16 * d, 1))
            v = nxt
        rows += v
    vt[...] = mm(jnp.concatenate(rows, axis=0), full_three)
    for e in range(8):
        v_ref[:, 64 * e : 64 * e + 64] = vt[pl.ds(e, 16, stride=8), :]

    for k in (1, 3, 6, 2, 5, 7, 8, 4):
        to = lax.rem(7 * lax.rem(label + CHIPS - k, CHIPS), CHIPS)
        send(4, v_ref, a_ref.at[k], (to * 2 + core, n))

    a_ref[0] = v_ref[...]
    await_all(rcv.at[4], a_ref.at[pl.ds(1, HALF)])
    partial = mm_rows(v_ref[...], a_ref[...].reshape(144, 512), ((1,), (1,)))
    row = lax.broadcasted_iota(jnp.int32, (8, 128), 0)
    for s in range(2):
        gp[s, 0:8] = partial[8 * s : 8 * s + 8, 0:128]
        last = jnp.concatenate([partial[8 * s : 8 * s + 8, 128:144]] * 8, axis=1)
        gp[s, 8:9] = jnp.sum(jnp.where(lane // 16 == lax.rem(8 - row, 8), last, 0.0), axis=0, keepdims=True)

    for to, peer in column_peers():
        send(5, gp.at[to, pl.ds(0, 9)], g3.at[core * NZ + n, pl.ds(0, 9)], peer)

    g3[core * NZ + n, 0:9] = gp[core, 0:9]
    await_all(rcv.at[5], g3.at[pl.ds(0, 2 * NZ - 1), pl.ds(0, 9)])
    for part in (slice(0, 8), slice(8, 9)):
        total = g3[0, part]
        for i in range(1, 2 * NZ):
            total = total + g3[i, part]
        gsum[part] = total * (1.0 / float(RANK * RANK * RANK_FOUR))

    for peer in plane_peers():
        send(6, gsum.at[pl.ds(0, 9)], gfull.at[slot, pl.ds(0, 9)], peer)

    gfull[slot, 0:9] = gsum[0:9]
    await_all(rcv.at[2], b0g.at[pl.ds(0, NW - 1)])
    basis_t = b0g[...].reshape(256, 64).T
    await_all(rcv.at[6], gfull.at[pl.ds(0, NW - 1), pl.ds(0, 9)])

    for i in range(CHIPS):
        at = 16 * (i % 8)
        for c in range(2):
            body = gfull[2 * i + c, 0:8]
            if at:
                body = pltpu.roll(body, at, 1)
            last = jnp.broadcast_to(gfull[2 * i + c, 8:9], (8, 128))
            last = pltpu.roll(last, 0, 1, stride=16, stride_axis=0)
            if at:
                last = pltpu.roll(last, at, 1)
            near = jnp.where(lane >= at, body, 0.0)
            far = jnp.where(lane < at, body, jnp.where(lane < at + 16, last, 0.0))
            half = i // 8
            rows = slice(16 * i + 8 * c, 16 * i + 8 * c + 8)
            gmat[rows, 128 * half : 128 * half + 128] = near
            gmat[rows, 128 - 128 * half : 256 - 128 * half] = far
    half_gram = gmat[...]
    row_block = lax.broadcasted_iota(jnp.int32, (256, 256), 0) // 16
    column_block = lax.broadcasted_iota(jnp.int32, (256, 256), 1) // 16
    held = lax.rem(column_block - row_block + CHIPS, CHIPS) <= HALF
    gram = split3(jnp.where(held, half_gram, half_gram.T))
    for i in range(3):
        gparts[i] = gram[i]
    zt_ref[...] = mm_parts(split3(basis_t), gram, ((1,), (0,)))

    @pl.loop(0, ITERS)
    def _(step):
        zt = zt_ref[...]
        z = split3(zt)
        below = [jnp.concatenate([jnp.zeros((64, 256), v.dtype), v], axis=0) for v in z]
        linv = inverse_cholesky(mm_parts(z, below, ((1,), (1,))))
        linv_ref[...] = linv
        image_t = mm_parts(z, [gparts[i] for i in range(3)], ((1,), (0,)))

        @pl.when(step < ITERS - 1)
        def _():
            zt_ref[...] = mm_rows(linv, image_t, ((1,), (0,)))

    z_ref[...] = zt_ref[...].T
    mine = z_ref[pl.ds(pl.multiple_of(slot * 8, 8), 8), :]
    out_ref[...] = mm(mine, linv_ref[...], ((1,), (1,))) * math.sqrt(256.0)

    await_all(snd.at[0], f2g.at[pl.ds(0, NW - 1)])
    await_all(snd.at[1], f3g.at[pl.ds(0, NZ - 1)])
    await_all(snd.at[2], b0g.at[pl.ds(0, NW - 1)])
    await_all(snd.at[3], r1.at[pl.ds(0, 2 * NZ - 1)])
    await_all(snd.at[4], a_ref.at[pl.ds(1, HALF)])
    await_all(snd.at[5], g3.at[pl.ds(0, 2 * NZ - 1), pl.ds(0, 9)])
    await_all(snd.at[6], gfull.at[pl.ds(0, NW - 1), pl.ds(0, 9)])


def per_device(tensor, factor_two, factor_three, factor_four, start_basis):
    f32, bf16 = jnp.float32, jnp.bfloat16
    x = tensor.reshape(8, 8, 128, 16, 4).transpose(0, 3, 1, 4, 2).reshape(4096, 128)
    hbm = pl.BlockSpec(memory_space=pltpu.HBM)
    operands = (x, factor_two, factor_three, factor_four.T, start_basis)
    return pl.pallas_call(
        kernel,
        out_shape=jax.ShapeDtypeStruct((8, 64), f32),
        in_specs=[hbm] * 5,
        out_specs=pl.BlockSpec(memory_space=pltpu.VMEM),
        scratch_shapes=[
            pltpu.VMEM((4096, 128), f32),
            pltpu.VMEM((32, 64), f32),
            pltpu.VMEM((16, 64), f32),
            pltpu.SMEM((2, 4), f32),
            pltpu.VMEM((8, 64), f32),
            pltpu.VMEM((16, 128), f32),
            pltpu.VMEM((NW, 16, 128), f32),
            pltpu.VMEM((NZ, 16, 64), f32),
            pltpu.VMEM((NW, 8, 64), f32),
            pltpu.VMEM((256, 1024), bf16),
            pltpu.VMEM((256, 1024), bf16),
            pltpu.VMEM((256, 1024), bf16),
            pltpu.VMEM((2, 8, 8, 128), f32),
            pltpu.VMEM((16, 8, 128), f32),
            pltpu.VMEM((128, 64), f32),
            pltpu.VMEM((16, 512), f32),
            pltpu.VMEM((HALF + 1, 16, 512), f32),
            pltpu.VMEM((2, 16, 128), f32),
            pltpu.VMEM((16, 16, 128), f32),
            pltpu.VMEM((16, 128), f32),
            pltpu.VMEM((NW, 16, 128), f32),
            pltpu.VMEM((256, 256), f32),
            pltpu.VMEM((3, 256, 256), bf16),
            pltpu.VMEM((64, 256), f32),
            pltpu.VMEM((256, 64), f32),
            pltpu.VMEM((64, 64), f32),
            pltpu.SemaphoreType.DMA((5,)),
            pltpu.SemaphoreType.DMA((7,)),
            pltpu.SemaphoreType.DMA((7,)),
        ],
        compiler_params=pltpu.CompilerParams(
            collective_id=0, has_side_effects=True, vmem_limit_bytes=40 * 2**20
        ),
        name="hooi",
    )(*(pltpu.with_memory_space_constraint(v, pltpu.HBM) for v in operands))


def solution(mesh):
    in_specs = (P("wa", None, "an", None), P("wa", None), P("an", None), P(), P("wa", None))
    return jax.shard_map(
        per_device, mesh=mesh, in_specs=in_specs, out_specs=P("wa", None), check_vma=False
    )
```
